256 devices in a mesh: patch: 64 (over x, z, y_hi), tensor: 4 (over y_lo, core).
Axes of the slice: x: 4, y: 4 (y_hi: 2, y_lo: 2; y = y_hi * 2 + y_lo), z: 8, core: 2. Of those that a mesh axis runs over, the one named last changes fastest.
Arguments:
- video: bfloat16 [17408, 3072], P('patch', 'tensor'), may hold values from -6 to 6
- positions: int32 [17408], P('patch'), may hold values from 0 to 17407, each once
- text_count: int32 [1], replicated, may hold values from 64 to 256
- mod_shift: float32 [3072], replicated, may hold values from -3 to 3
- mod_scale: float32 [3072], replicated, may hold values from -3 to 3
- gate: float32 [3072], P('tensor'), may hold values from 0.5 to 4
- w_query: bfloat16 [3072, 1536], P(None, 'tensor'), may hold values from -0.109375 to 0.109375
- w_key: bfloat16 [3072, 1536], P(None, 'tensor'), may hold values from -0.109375 to 0.109375
- w_value: bfloat16 [3072, 1536], P(None, 'tensor'), may hold values from -0.109375 to 0.109375
- w_out: bfloat16 [1536, 3072], P('tensor'), may hold values from -0.15625 to 0.15625
- q_gain: float32 [128], replicated, may hold values from 0.5 to 1.5
- k_gain: float32 [128], replicated, may hold values from 1.5 to 4
- stale_keys: bfloat16 [17408, 1536], P('patch', 'tensor'), as said below
- stale_values: bfloat16 [17408, 1536], P('patch', 'tensor'), may hold values from -6 to 6
- text_keys: bfloat16 [256, 1536], P(None, 'tensor'), may hold values from -16 to 16
- text_values: bfloat16 [256, 1536], P(None, 'tensor'), may hold values from -6 to 6
Outputs:
- mixed: float32 [17408, 3072], P('patch', 'tensor')
- fresh_keys: bfloat16 [17408, 1536], P('patch', 'tensor')
- fresh_values: bfloat16 [17408, 1536], P('patch', 'tensor')
The draws below stay inside these ranges and needn't reach their ends.
Inputs may be any that keep to these rules, and one draw needn't show every extreme that they name: `positions`: each token's place in the clip, counted frame by frame, row by row; every place occurs once. Text slots from text_count on are padding. `stale_keys`: keys of the previous denoising step.
All inputs are finite; a program needn't handle non-finite values.
Results may differ from the reference program's by a relative error of at most 0.013.
The reference program's roundings to bfloat16 on the way (of `normed`, `rounded` and `attended`) count: a program that leaves them out, or rounds other values in their place, can miss the bound.
Values may be sent and summed in bfloat16 or wider, within the bound.
A program may use at most 128 MiB of HBM per device.

```python
import math
import jax
import jax.numpy as jnp
from jax import lax

D = 3072
HEADS = 12
HEAD_DIM = 128
TEXT = 256
GRID_H = 45
GRID_W = 80
TOK_DEV = 272
TOKENS = 17408
N_PATCH = 64


def draw_stale_keys(key, part):
    key = jax.random.fold_in(key, 7)
    first_key = jax.random.fold_in(key, 0)
    base = 2.5 * jnp.clip(jax.random.normal(first_key, (TOKENS, HEADS * HEAD_DIM), jnp.float32), -6.0, 6.0)
    return base.astype(jnp.bfloat16)


def steps_of(key, shape, cuts, smallest, top_value):
    gain, own = 1.0, jax.random.fold_in(key, 6)
    for dim, parts in cuts:
        draws = jnp.exp(jax.random.uniform(jax.random.fold_in(own, dim), (parts,), jnp.float32, smallest / len(cuts), top_value / len(cuts)))
        gain = gain * jnp.repeat(draws, shape[dim] // parts).reshape([-1 if axis == dim else 1 for axis in range(len(shape))])
    return gain


def noise(own_key, shape, scale, most, pieces=(), held_as=jnp.bfloat16):
    values = scale * jax.random.normal(own_key, shape, jnp.float32)
    if pieces:
        values = values * steps_of(own_key, shape, pieces, -0.22, 0.18)
    return jnp.clip(values, -most, most).astype(held_as)


def setup_inputs(seed: int = 0) -> dict:
    arg_keys = jax.random.split(jax.random.key(seed), 17)
    video = noise(arg_keys[0], (TOKENS, D), 1.0, 6.0, ((0, 64), (1, 4)))
    positions = jax.random.permutation(arg_keys[1], TOKENS).astype(jnp.int32)
    text_count = jax.random.randint(arg_keys[2], (1,), TEXT // 4, TEXT + 1).astype(jnp.int32)
    mod_shift = noise(arg_keys[3], (D,), 0.5, 3.0, (), jnp.float32)
    mod_scale = noise(arg_keys[4], (D,), 0.5, 3.0, (), jnp.float32)
    gate = jnp.clip(jnp.exp(math.log(4.0) - 2.0794415 * jax.random.uniform(arg_keys[5], (D,), jnp.float32) ** steps_of(arg_keys[5], (D,), ((0, 4),), -0.2, 0.2)), 0.5, 4.0)
    w_query = noise(arg_keys[6], (D, HEADS * HEAD_DIM), D ** -0.5, 0.109375, ((1, 4),))
    w_key = noise(arg_keys[7], (D, HEADS * HEAD_DIM), D ** -0.5, 0.109375, ((1, 4),))
    w_value = noise(arg_keys[8], (D, HEADS * HEAD_DIM), D ** -0.5, 0.109375, ((1, 4),))
    w_out = noise(arg_keys[9], (HEADS * HEAD_DIM, D), (HEADS * HEAD_DIM) ** -0.5, 0.15625, ((0, 4),))
    q_gain = jnp.clip(1.0 + 0.1 * jax.random.normal(arg_keys[10], (HEAD_DIM,), jnp.float32), 0.5, 1.5)
    k_gain = jnp.clip(jnp.exp(jax.random.uniform(arg_keys[11], (HEAD_DIM,), jnp.float32, math.log(1.5), math.log(4.0))), 1.5, 4.0)
    stale_keys = draw_stale_keys(jax.random.fold_in(arg_keys[16], 71), 0)
    stale_values = noise(arg_keys[13], (TOKENS, HEADS * HEAD_DIM), 1.0, 6.0, ((0, 64), (1, 4)))
    text_keys = noise(arg_keys[14], (TEXT, HEADS * HEAD_DIM), 2.5, 16.0, ((1, 4),))
    text_values = noise(arg_keys[15], (TEXT, HEADS * HEAD_DIM), 1.0, 6.0, ((1, 4),))
    return dict(video=video, positions=positions, text_count=text_count, mod_shift=mod_shift, mod_scale=mod_scale, gate=gate, w_query=w_query, w_key=w_key, w_value=w_value, w_out=w_out, q_gain=q_gain, k_gain=k_gain, stale_keys=stale_keys, stale_values=stale_values, text_keys=text_keys, text_values=text_values)


EPSILON = 1e-06

def modulate(video, mod_shift, mod_scale):
    values = video.astype(jnp.float32)
    center = lax.optimization_barrier(jnp.mean(values, axis=1, keepdims=True))
    spread = lax.optimization_barrier(jnp.mean((values - center) ** 2, axis=1, keepdims=True))
    return ((values - center) * lax.rsqrt(spread + EPSILON) * (1.0 + mod_scale) + mod_shift).astype(jnp.bfloat16)

def head_norm(vectors, norm_gain):
    return vectors * lax.rsqrt(lax.optimization_barrier(jnp.mean(vectors * vectors, axis=-1, keepdims=True)) + EPSILON) * norm_gain

def rotate(vectors, positions):
    head_size = vectors.shape[-1]
    pair_count = head_size // 2
    time_pairs = head_size // 16
    height_pairs = (pair_count - time_pairs) // 2
    width_pairs = pair_count - time_pairs - height_pairs
    frame = (positions // (GRID_H * GRID_W)).astype(jnp.float32)
    height = (positions // GRID_W % GRID_H).astype(jnp.float32)
    across = (positions % GRID_W).astype(jnp.float32)

    def rates(number):
        return 256.0 ** (-jnp.arange(number, dtype=jnp.float32) / number)
    angles = jnp.concatenate([frame[:, None] * rates(time_pairs)[None, :], height[:, None] * rates(height_pairs)[None, :], across[:, None] * rates(width_pairs)[None, :]], axis=1)
    cosine = jnp.cos(angles)[:, None, :]
    sine = jnp.sin(angles)[:, None, :]
    paired = vectors.reshape(vectors.shape[:-1] + (pair_count, 2))
    first_half = paired[..., 0]
    second_half = paired[..., 1]
    turned = jnp.stack([first_half * cosine - second_half * sine, first_half * sine + second_half * cosine], axis=-1)
    return turned.reshape(vectors.shape)

def project_heads(normed, weight, norm_gain, positions):
    heads = jnp.dot(normed, weight, preferred_element_type=jnp.float32)
    heads = heads.reshape(heads.shape[0], -1, HEAD_DIM)
    return lax.optimization_barrier(rotate(head_norm(heads, norm_gain), positions).astype(jnp.bfloat16))

def reference(video, positions, text_count, mod_shift, mod_scale, gate, w_query, w_key, w_value, w_out, q_gain, k_gain, stale_keys, stale_values, text_keys, text_values):
    normed = modulate(video, mod_shift, mod_scale)
    queries = project_heads(normed, w_query, q_gain, positions)
    fresh_keys = project_heads(normed, w_key, k_gain, positions).reshape(TOKENS, HEADS * HEAD_DIM)
    fresh_values = lax.optimization_barrier(jnp.dot(normed, w_value, preferred_element_type=jnp.float32).astype(jnp.bfloat16))
    text_live = jnp.arange(TEXT, dtype=jnp.int32) < text_count[0]
    live_keys = jnp.concatenate([jnp.ones((TOKENS,), dtype=bool), text_live])
    factor = 1.0 / math.sqrt(HEAD_DIM)

    def one_block(block):
        start = (block * TOK_DEV).astype(jnp.int32)
        own_keys = lax.dynamic_slice_in_dim(fresh_keys, start, TOK_DEV, 0)
        own_values = lax.dynamic_slice_in_dim(fresh_values, start, TOK_DEV, 0)
        block_keys = lax.dynamic_update_slice_in_dim(stale_keys, own_keys, start, 0)
        block_values = lax.dynamic_update_slice_in_dim(stale_values, own_values, start, 0)
        all_keys = jnp.concatenate([block_keys, text_keys], axis=0).reshape(-1, HEADS, HEAD_DIM).astype(jnp.float32)
        all_values = jnp.concatenate([block_values, text_values], axis=0).reshape(-1, HEADS, HEAD_DIM).astype(jnp.float32)
        block_queries = lax.dynamic_slice_in_dim(queries, start, TOK_DEV, 0).astype(jnp.float32)
        scores = jnp.einsum('qhd,khd->hqk', block_queries, all_keys) * factor
        scores = jnp.where(live_keys[None, None, :], scores, -1e+30)
        top_score = lax.optimization_barrier(jnp.max(scores, axis=-1, keepdims=True))
        weights = jnp.where(live_keys[None, None, :], jnp.exp(scores - top_score), 0.0)
        totals = lax.optimization_barrier(jnp.sum(weights, axis=-1))
        rounded = lax.optimization_barrier(weights.astype(jnp.bfloat16)).astype(jnp.float32)
        summed = jnp.einsum('hqk,khd->qhd', rounded, all_values)
        return (summed / jnp.transpose(totals)[:, :, None]).astype(jnp.bfloat16)
    attended = lax.map(one_block, jnp.arange(N_PATCH, dtype=jnp.int32))
    attended = attended.reshape(TOKENS, HEADS * HEAD_DIM)
    branch = jnp.dot(attended, w_out, preferred_element_type=jnp.float32)
    mixed = video.astype(jnp.float32) + gate * branch
    return (mixed, fresh_keys, fresh_values)
```

```python
import math

import jax
import jax.numpy as jnp
import numpy as np
from jax import lax
from jax.experimental import pallas as pl
from jax.experimental.pallas import tpu as pltpu
from jax.sharding import PartitionSpec as P

D = 3072
HEAD_DIM = 128
LOCAL_HEADS = 3
ROWS = 272
WIDTH = LOCAL_HEADS * HEAD_DIM
FEAT = 768
TEXT = 256
EPSILON = 1e-06
EXP_FACTOR = math.log2(math.e) / math.sqrt(HEAD_DIM)

FRESH = TEXT
OTHERS = TEXT + ROWS
AT = {1: OTHERS, 7: OTHERS + ROWS, 2: OTHERS + 2 * ROWS, 6: OTHERS + 3 * ROWS,
      3: OTHERS + 4 * ROWS, 5: OTHERS + 5 * ROWS, 4: OTHERS + 6 * ROWS}
EARLY = OTHERS + 4 * ROWS
OWN_STALE = OTHERS + 7 * ROWS
KEYS = OTHERS + 8 * ROWS

HALVES = ((0, 144), (144, 128))

R_SIB, R_PART, R_FWD, R_KV, R_Q, R_WO, R_RS, R_ATT = 0, 2, 4, 6, 22, 31, 35, 51
N_RECV = 54
N_SEND = 64
N_LOCAL = 16


def pair_rates():
    pairs = HEAD_DIM // 2
    frame = HEAD_DIM // 16
    high = (pairs - frame) // 2
    wide = pairs - frame - high
    rates = np.concatenate(
        [256.0 ** (-np.arange(n, dtype=np.float64) / n) for n in (frame, high, wide)]
    )
    return np.repeat(rates, 2).astype(np.float32)[None, :]


def kernel(
    video, pos, count, shift, scale, gate, wq, wk, wv, wout, q_gain, k_gain, sk, sv, tk, tv, rates,
    mixed, fk, fv,
    vb, nb, wqb, wkb, wvb, kb, vvb, qb, cosb, sinb, ob, st, so, ss, ro, rs, wob, atb,
    ssem, rsem, lsem,
):
    f32 = jnp.float32
    p = lax.axis_index("patch")
    t = lax.axis_index("tensor")
    x = p // 16
    z = (p // 2) % 8
    yh = p % 2
    yl = t // 2
    c = t % 2
    turn = 2 * yl
    u = (x - turn + 7) % 4
    ring_place = u * (1 - yh) + (7 - u) * yh

    def along_z(step):
        return x * 16 + ((z + step + 8) % 8) * 2 + yh

    def around(step):
        place = (ring_place + step + 8) % 8
        nyh = place // 4
        nu = place * (1 - nyh) + (7 - place) * nyh
        nx = (turn + 1 + nu) % 4
        return nx * 16 + z * 2 + nyh

    z_next, z_prev, w_next, w_prev = along_z(1), along_z(-1), around(1), around(-1)
    kv_next = (c * z_next + (1 - c) * w_next, t)
    kv_prev = (c * z_prev + (1 - c) * w_prev, t)
    q_next = (c * w_next + (1 - c) * z_next, t)
    q_prev = (c * w_prev + (1 - c) * z_prev, t)
    t_sib = yl * 2 + 1 - c
    t_part = (1 - yl) * 2 + c
    t_far0 = (1 - yl) * 2
    t_far1 = (1 - yl) * 2 + 1
    p_flip = p + 1 - 2 * yh
    sibling = (p, t_sib)
    partner = (p, t_part)
    t_cross = (1 - yl) * 2 + 1 - c

    local = []

    def fetch(src, dst):
        copy = pltpu.make_async_copy(src, dst, lsem.at[len(local)])
        copy.start()
        local.append(copy)
        return copy

    own_video = fetch(video, vb.at[t])
    own_copies = [
        fetch(sk, kb.at[pl.ds(OWN_STALE, ROWS)]),
        fetch(sv, vvb.at[pl.ds(OWN_STALE, ROWS)]),
        fetch(tk, kb.at[pl.ds(0, TEXT)]),
        fetch(tv, vvb.at[pl.ds(0, TEXT)]),
    ]
    got_wq = fetch(wq, wqb)
    got_wk = fetch(wk, wkb)
    got_wv = fetch(wv, wvb)
    got_wo = fetch(wout.at[:, pl.ds(pl.multiple_of(t * FEAT, FEAT), FEAT)], wob.at[t])

    barrier = pltpu.get_barrier_semaphore()
    greeted = (
        sibling, (p, t_far0), (p, t_far1), (p_flip, t_far0), (p_flip, t_far1),
        kv_next, kv_prev, q_next, q_prev,
    )
    for device in greeted:
        pl.semaphore_signal(barrier, inc=1, device_id=device, device_id_type=pl.DeviceIdType.MESH)
    pl.semaphore_wait(barrier, len(greeted))

    sent = []

    def send(src, dst, recv, device):
        index = len(sent)

        def make():
            return pltpu.make_async_remote_copy(
                src_ref=src() if callable(src) else src, dst_ref=dst() if callable(dst) else dst,
                send_sem=ssem.at[index], recv_sem=rsem.at[recv],
                device_id=device, device_id_type=pl.DeviceIdType.MESH,
            )

        sent.append(make)
        make().start()

    def arrived(dst, recv):
        pltpu.make_async_copy(dst, dst, rsem.at[recv]).wait()

    for half, (r0, n) in enumerate(HALVES):
        send(video.at[pl.ds(r0, n)], vb.at[t, pl.ds(r0, n)], R_PART + half, partner)
    for half, (r0, n) in enumerate(HALVES):
        send(video.at[pl.ds(r0, n)], vb.at[t, pl.ds(r0, n)], R_SIB + half, sibling)

    def kv_slot(buffer, d):
        return buffer.at[pl.ds(AT[d], ROWS)]

    send(sk, kv_slot(kb, 7), R_KV + 14, kv_next)
    send(sk, kv_slot(kb, 1), R_KV + 2, kv_prev)
    send(sv, kv_slot(vvb, 7), R_KV + 15, kv_next)
    send(sv, kv_slot(vvb, 1), R_KV + 3, kv_prev)

    def kv_pass(came, going, target, buffer, which):
        arrived(kv_slot(buffer, came), R_KV + 2 * came + which)
        if going is not None:
            send(kv_slot(buffer, came), kv_slot(buffer, going), R_KV + 2 * going + which, target)

    row_id = lax.broadcasted_iota(jnp.int32, (ROWS, ROWS), 0)
    col_id = lax.broadcasted_iota(jnp.int32, (ROWS, ROWS), 1)
    place = jnp.sum(jnp.where(row_id == col_id, pos[...].astype(f32), 0.0), axis=1, keepdims=True)
    frame = jnp.floor((place + 0.5) * (1.0 / 3600.0))
    within = place - 3600.0 * frame
    high = jnp.floor((within + 0.5) * (1.0 / 80.0))
    across = within - 80.0 * high
    lane = lax.broadcasted_iota(jnp.int32, (ROWS, HEAD_DIM), 1)
    angle = jnp.where(lane < 16, frame, jnp.where(lane < 72, high, across)) * rates[...]
    even = lane % 2 == 0
    cosb[...] = jnp.cos(angle)
    sine = jnp.sin(angle)
    sinb[...] = jnp.where(even, -sine, sine)

    def normalise(r0, n):
        blocks = [vb[f, r0 : r0 + n, :].astype(f32) for f in range(4)]
        mean = sum(jnp.sum(b, axis=1, keepdims=True) for b in blocks) * (1.0 / D)
        spread = sum(jnp.sum((b - mean) ** 2, axis=1, keepdims=True) for b in blocks) * (1.0 / D)
        rstd = lax.rsqrt(spread + EPSILON)
        for f in range(4):
            cols = slice(f * FEAT, (f + 1) * FEAT)
            nb[r0 : r0 + n, cols] = (
                (blocks[f] - mean) * rstd * (1.0 + scale[:, cols]) + shift[:, cols]
            ).astype(jnp.bfloat16)

    def rows_of(slot, half):
        r0, n = HALVES[half]
        return vb.at[slot, pl.ds(r0, n)]

    own_video.wait()
    for half in range(2):
        arrived(rows_of(t_part, half), R_PART + half)
        send(rows_of(t_part, half), rows_of(t_part, half), R_FWD + half, sibling)
        if half == 0:
            kv_pass(7, 6, kv_next, kb, 0)
            kv_pass(1, 2, kv_prev, kb, 0)
            kv_pass(7, 6, kv_next, vvb, 1)
            kv_pass(1, 2, kv_prev, vvb, 1)
    for half in range(2):
        arrived(rows_of(t_sib, half), R_SIB + half)
        arrived(rows_of(t_cross, half), R_FWD + half)
        normalise(*HALVES[half])

    def project(weight, gain, target):
        flat = jnp.dot(nb[...], weight[...], preferred_element_type=f32)
        for h in range(LOCAL_HEADS):
            hs = slice(h * HEAD_DIM, (h + 1) * HEAD_DIM)
            v = flat[:, hs]
            v = v * lax.rsqrt(jnp.mean(v * v, axis=1, keepdims=True) + EPSILON) * gain[...]
            other = jnp.where(even, pltpu.roll(v, HEAD_DIM - 1, 1), pltpu.roll(v, 1, 1))
            target[:, hs] = (v * cosb[...] + other * sinb[...]).astype(jnp.bfloat16)

    got_wq.wait()
    project(wqb, q_gain, qb.at[0])
    send(qb.at[0], qb.at[7], R_Q + 7, q_next)
    send(qb.at[0], qb.at[1], R_Q + 1, q_prev)

    send(
        wout.at[:, pl.ds(pl.multiple_of(t_sib * FEAT, FEAT), FEAT)], wob.at[t], R_WO + t, sibling
    )
    send(
        wout.at[:, pl.ds(pl.multiple_of(t_far0 * FEAT, FEAT), FEAT)], wob.at[t], R_WO + t, (p, t_far0)
    )
    send(
        wout.at[:, pl.ds(pl.multiple_of(t_far1 * FEAT, FEAT), FEAT)], wob.at[t], R_WO + t,
        (p_flip, t_far1),
    )

    kv_pass(6, 5, kv_next, kb, 0)
    kv_pass(2, 3, kv_prev, kb, 0)
    kv_pass(6, 5, kv_next, vvb, 1)
    kv_pass(2, 3, kv_prev, vvb, 1)

    got_wk.wait()
    project(wkb, k_gain, kb.at[pl.ds(FRESH, ROWS)])
    got_wv.wait()
    vvb[FRESH : FRESH + ROWS, :] = jnp.dot(nb[...], wvb[...], preferred_element_type=f32).astype(
        jnp.bfloat16
    )
    out_k = fetch(kb.at[pl.ds(FRESH, ROWS)], fk)
    out_v = fetch(vvb.at[pl.ds(FRESH, ROWS)], fv)
    for copy in own_copies:
        copy.wait()

    def scores_of(j, h, k0, n):
        hs = slice(h * HEAD_DIM, (h + 1) * HEAD_DIM)
        return lax.dot_general(
            qb[j, :, hs], kb[k0 : k0 + n, hs], (((1,), (1,)), ((), ())), preferred_element_type=f32
        )

    def product(weights, h, k0, n):
        hs = slice(h * HEAD_DIM, (h + 1) * HEAD_DIM)
        return jnp.dot(
            weights.astype(jnp.bfloat16), vvb[k0 : k0 + n, hs], preferred_element_type=f32
        )

    def keep(j, h, top, total, summed):
        ob[j, :, h * HEAD_DIM : (h + 1) * HEAD_DIM] = summed
        st[j, 0:ROWS, h : h + 1] = top
        st[j, 0:ROWS, 3 + h : 4 + h] = total

    text_rows = lax.broadcasted_iota(jnp.int32, (1, EARLY), 1)
    live = (text_rows < count[0]) | (text_rows >= TEXT)
    for h in range(LOCAL_HEADS):
        scores = jnp.where(live, scores_of(0, h, 0, EARLY), -1e30)
        top = jnp.max(scores, axis=1, keepdims=True)
        weights = jnp.exp2((scores - top) * EXP_FACTOR)
        keep(0, h, top, jnp.sum(weights, axis=1, keepdims=True), product(weights, h, 0, EARLY))

    kv_pass(5, 4, kv_next, kb, 0)
    kv_pass(3, 4, kv_prev, vvb, 1)
    kv_pass(5, None, None, vvb, 1)
    kv_pass(3, None, None, kb, 0)

    def q_pass(came, going, target):
        arrived(qb.at[came], R_Q + came)
        if going is not None:
            send(lambda: qb.at[came], lambda: qb.at[going], R_Q + going, target)

    q_pass(7, 6, q_next)
    q_pass(1, 2, q_prev)
    kv_pass(4, None, None, kb, 0)
    kv_pass(4, None, None, vvb, 1)

    def merge(j, slot, r0, n):
        rows = slice(r0, r0 + n)
        stats = jnp.transpose(rs[slot])[rows, :]
        for h in range(LOCAL_HEADS):
            hs = slice(h * HEAD_DIM, (h + 1) * HEAD_DIM)
            top_a, top_b = st[j, rows, h : h + 1], stats[:, h : h + 1]
            total_a, total_b = st[j, rows, 3 + h : 4 + h], stats[:, 3 + h : 4 + h]
            top = jnp.maximum(top_a, top_b)
            part_a = jnp.exp2((top_a - top) * EXP_FACTOR)
            part_b = jnp.exp2((top_b - top) * EXP_FACTOR)
            ob[j, rows, hs] = ob[j, rows, hs] * part_a + ro[slot, rows, hs].astype(f32) * part_b
            st[j, rows, h : h + 1] = top
            st[j, rows, 3 + h : 4 + h] = total_a * part_a + total_b * part_b

    def pack(j):
        so[j] = ob[j].astype(jnp.bfloat16)
        ss[j] = jnp.transpose(st[j])[0:8, :]

    def received(slot, r0=0, n=ROWS):
        arrived(ro.at[slot, pl.ds(r0, n)], R_RS + 2 * slot)
        arrived(rs.at[slot], R_RS + 2 * slot + 1)

    def emit(j, slot, target, r0=0, n=ROWS):
        send(
            lambda: so.at[j, pl.ds(r0, n)], lambda: ro.at[slot, pl.ds(r0, n)], R_RS + 2 * slot,
            target,
        )
        send(lambda: ss.at[j], lambda: rs.at[slot], R_RS + 2 * slot + 1, target)

    st[...] = jnp.where(
        lax.broadcasted_iota(jnp.int32, st.shape, 0) == 0, st[...], jnp.zeros(st.shape, f32)
    )

    def step(i, order):
        j = order % 8

        @pl.when(i == 1)
        def _():
            q_pass(6, 5, q_next)
            q_pass(2, 3, q_prev)

        @pl.when(i == 2)
        def _():
            arrived(qb.at[5], R_Q + 5)
            send(
                lambda: qb.at[5, pl.ds(0, 144)], lambda: qb.at[4, pl.ds(0, 144)], R_Q + 4, q_next
            )
            arrived(qb.at[3], R_Q + 3)
            send(
                lambda: qb.at[3, pl.ds(144, 128)], lambda: qb.at[4, pl.ds(144, 128)], R_Q + 8, q_prev
            )

        @pl.when(i == 3)
        def _():
            arrived(qb.at[4, pl.ds(0, 144)], R_Q + 4)
            arrived(qb.at[4, pl.ds(144, 128)], R_Q + 8)

        for h in range(LOCAL_HEADS):
            scores = scores_of(j, h, OTHERS, 8 * ROWS)
            top = jnp.max(scores, axis=1, keepdims=True)
            weights = jnp.exp2((scores - top) * EXP_FACTOR)
            keep(
                j, h, top, jnp.sum(weights, axis=1, keepdims=True),
                product(weights, h, OTHERS, 8 * ROWS),
            )

        @pl.when(i == 3)
        def _():
            pack(4)
            emit(4, 3, q_next, 0, 144)
            emit(4, 5, q_prev, 144, 128)

        @pl.when(i == 4)
        def _():
            received(3, 0, 144)
            merge(3, 3, 0, 144)
            pack(3)
            emit(3, 2, q_next)
            received(5, 144, 128)
            merge(5, 5, 144, 128)
            pack(5)
            emit(5, 6, q_prev)

        @pl.when(i == 5)
        def _():
            received(2)
            merge(2, 2, 0, ROWS)
            pack(2)
            emit(2, 1, q_next)

        @pl.when(i == 6)
        def _():
            received(6)
            merge(6, 6, 0, ROWS)
            pack(6)
            emit(6, 7, q_prev)
            received(1)
            merge(1, 1, 0, ROWS)
            pack(1)
            emit(1, 0, q_next)

        return order // 8

    lax.fori_loop(0, 7, step, jnp.int32(0o6254371))

    for h in range(LOCAL_HEADS):
        hs = slice(h * HEAD_DIM, (h + 1) * HEAD_DIM)
        n = OWN_STALE - EARLY
        scores = scores_of(0, h, EARLY, n)
        before = st[0, 0:ROWS, h : h + 1]
        top = jnp.maximum(before, jnp.max(scores, axis=1, keepdims=True))
        weights = jnp.exp2((scores - top) * EXP_FACTOR)
        old = jnp.exp2((before - top) * EXP_FACTOR)
        total = st[0, 0:ROWS, 3 + h : 4 + h] * old + jnp.sum(weights, axis=1, keepdims=True)
        keep(0, h, top, total, ob[0, :, hs] * old + product(weights, h, EARLY, n))

    received(7)
    merge(7, 7, 0, ROWS)
    pack(7)
    emit(7, 4, q_prev)
    received(0)
    merge(0, 0, 0, ROWS)
    received(4)
    merge(0, 4, 0, ROWS)

    for h in range(LOCAL_HEADS):
        hs = slice(h * HEAD_DIM, (h + 1) * HEAD_DIM)
        atb[t, :, hs] = (ob[0, :, hs] / st[0, 0:ROWS, 3 + h : 4 + h]).astype(jnp.bfloat16)

    send(atb.at[t], atb.at[t], R_ATT + 1, partner)
    send(atb.at[t], atb.at[t], R_ATT, sibling)
    got_wo.wait()
    for slot in (t_sib, t_far0, t_far1):
        arrived(wob.at[slot], R_WO + slot)

    def term(slot):
        return jnp.dot(atb[slot], wob[slot], preferred_element_type=f32)

    branch = term(t)
    arrived(atb.at[t_sib], R_ATT)
    branch = branch + term(t_sib)
    arrived(atb.at[t_part], R_ATT + 1)
    send(atb.at[t_part], atb.at[t_part], R_ATT + 2, sibling)
    branch = branch + term(t_part)
    arrived(atb.at[t_cross], R_ATT + 2)
    branch = branch + term(t_cross)
    mixed[...] = vb[t].astype(f32) + gate[...] * branch

    out_k.wait()
    out_v.wait()
    for make in sent:
        make().wait_send()


def shards(
    video, positions, text_count, mod_shift, mod_scale, gate, w_query, w_key, w_value, w_out,
    q_gain, k_gain, stale_keys, stale_values, text_keys, text_values,
):
    bf16, f32 = jnp.bfloat16, jnp.float32
    vmem = pl.BlockSpec(memory_space=pltpu.VMEM)
    smem = pl.BlockSpec(memory_space=pltpu.SMEM)
    hbm = pl.BlockSpec(memory_space=pl.ANY)
    return pl.pallas_call(
        kernel,
        out_shape=(
            jax.ShapeDtypeStruct((ROWS, FEAT), f32),
            jax.ShapeDtypeStruct((ROWS, WIDTH), bf16),
            jax.ShapeDtypeStruct((ROWS, WIDTH), bf16),
        ),
        in_specs=[
            hbm, vmem, smem, vmem, vmem, vmem, hbm, hbm, hbm, hbm, vmem, vmem, hbm, hbm, hbm, hbm,
            vmem,
        ],
        out_specs=(vmem, hbm, hbm),
        scratch_shapes=[
            pltpu.VMEM((4, ROWS, FEAT), bf16),
            pltpu.VMEM((ROWS, D), bf16),
            pltpu.VMEM((D, WIDTH), bf16),
            pltpu.VMEM((D, WIDTH), bf16),
            pltpu.VMEM((D, WIDTH), bf16),
            pltpu.VMEM((KEYS, WIDTH), bf16),
            pltpu.VMEM((KEYS, WIDTH), bf16),
            pltpu.VMEM((8, ROWS, WIDTH), bf16),
            pltpu.VMEM((ROWS, HEAD_DIM), f32),
            pltpu.VMEM((ROWS, HEAD_DIM), f32),
            pltpu.VMEM((8, ROWS, WIDTH), f32),
            pltpu.VMEM((8, 384, HEAD_DIM), f32),
            pltpu.VMEM((8, ROWS, WIDTH), bf16),
            pltpu.VMEM((8, 8, 384), f32),
            pltpu.VMEM((8, ROWS, WIDTH), bf16),
            pltpu.VMEM((8, 8, 384), f32),
            pltpu.VMEM((4, WIDTH, FEAT), bf16),
            pltpu.VMEM((4, ROWS, WIDTH), bf16),
            pltpu.SemaphoreType.DMA((N_SEND,)),
            pltpu.SemaphoreType.DMA((N_RECV,)),
            pltpu.SemaphoreType.DMA((N_LOCAL,)),
        ],
        compiler_params=pltpu.CompilerParams(
            collective_id=0, has_side_effects=True, vmem_limit_bytes=60 * 1024 * 1024
        ),
        name="attention_half",
    )(
        video,
        positions.reshape(1, ROWS),
        text_count,
        mod_shift.reshape(1, D),
        mod_scale.reshape(1, D),
        gate.reshape(1, FEAT),
        w_query,
        w_key,
        w_value,
        w_out,
        q_gain.reshape(1, HEAD_DIM),
        k_gain.reshape(1, HEAD_DIM),
        stale_keys,
        stale_values,
        text_keys,
        text_values,
        jnp.asarray(pair_rates()),
    )


def solution(mesh):
    return jax.shard_map(
        shards,
        mesh=mesh,
        in_specs=(
            P("patch", "tensor"),
            P("patch"),
            P(),
            P(),
            P(),
            P("tensor"),
            P(None, "tensor"),
            P(None, "tensor"),
            P(None, "tensor"),
            P("tensor", None),
            P(),
            P(),
            P("patch", "tensor"),
            P("patch", "tensor"),
            P(None, "tensor"),
            P(None, "tensor"),
        ),
        out_specs=(P("patch", "tensor"), P("patch", "tensor"), P("patch", "tensor")),
        check_vma=False,
    )
```

```python
import functools
import math

import jax
import jax.numpy as jnp
import numpy as np
from jax import lax
from jax.experimental import pallas as pl
from jax.experimental.pallas import tpu as pltpu
from jax.sharding import PartitionSpec as P

D = 3072
HEAD_DIM = 128
LOCAL_HEADS = 3
ROWS = 272
WIDTH = LOCAL_HEADS * HEAD_DIM
FEAT = 768
TEXT = 256
EPSILON = 1e-06
EXP_FACTOR = math.log2(math.e) / math.sqrt(HEAD_DIM)

NEAR = TEXT
FRESH = NEAR + 4 * ROWS
FAR = FRESH + ROWS
OWN_STALE = FAR + 3 * ROWS
KEYS = OWN_STALE + ROWS
SPAN = 4 * ROWS

HALVES = ((0, 144), (144, 128))

STEPS = (
    (0, 0), (1, 0), (2, 0), (3, 0), (4, 0), (1, 1), (2, 1), (5, 0),
    (5, 1), (6, 0), (6, 1), (7, 0), (7, 1), (3, 1), (4, 1), (0, 1),
)
Z_STEP = {1: -1, 2: 1, 3: -2, 4: 2, 5: -3, 6: 3, 7: 4}
X_STEP = {1: (-1, 0), 2: (1, 0), 3: (2, 0), 4: (0, 1), 5: (-1, 1), 6: (1, 1), 7: (2, 1)}


def digits(values, base):
    total = 0
    for value in reversed(values):
        total = total * base + value
    return total


def step_codes(first):
    part = STEPS[first : first + 8]
    return (
        digits([slot for slot, _ in part], 8),
        digits([half for _, half in part], 2),
        digits([Z_STEP.get(slot, 0) + 3 for slot, _ in part], 8),
        digits([X_STEP.get(slot, (0, 0))[0] + 1 + 4 * X_STEP.get(slot, (0, 0))[1] for slot, _ in part], 8),
    )


R_SIB, R_PART, R_FWD, R_KV, R_Q, R_WO, R_RS, R_ATT = 0, 2, 4, 6, 22, 30, 34, 50
N_RECV = 53
N_SEND = 64
N_LOCAL = 16


def pair_rates():
    pairs = HEAD_DIM // 2
    frame = HEAD_DIM // 16
    high = (pairs - frame) // 2
    wide = pairs - frame - high
    rates = np.concatenate(
        [256.0 ** (-np.arange(n, dtype=np.float64) / n) for n in (frame, high, wide)]
    )
    return np.repeat(rates, 2).astype(np.float32)[None, :]


def kernel(
    video, pos, count, shift, scale, gate, wq, wk, wv, wout, q_gain, k_gain, sk, sv, tk, tv, rates,
    mixed, fk, fv,
    vb, nb, wqb, wkb, wvb, kb, vvb, qb, posb, cosb, sinb, sb, ob, tops, sums, stp, so, ss, ro, rs, wob, atb,
    ssem, osem, rsem, lsem,
):
    f32 = jnp.float32
    bf16 = jnp.bfloat16
    p = lax.axis_index("patch")
    t = lax.axis_index("tensor")
    x = p // 16
    z = (p // 2) % 8
    yh = p % 2
    yl = t // 2
    c = t % 2

    def along_z(step):
        return x * 16 + ((z + step + 8) % 8) * 2 + yh

    def along_x(step, flip):
        return ((x + step + 4) % 4) * 16 + z * 2 + yh + flip * (1 - 2 * yh)

    on_z = (along_z(1), along_z(-1), along_z(2), along_z(-2))
    on_x = (along_x(1, 0), along_x(-1, 0), along_x(2, 0), along_x(0, 1))
    k1, k2, k3, k4 = ((c * a + (1 - c) * b, t) for a, b in zip(on_z, on_x))
    q1, q2, q3, q4 = ((c * b + (1 - c) * a, t) for a, b in zip(on_z, on_x))
    t_sib = yl * 2 + 1 - c
    t_part = (1 - yl) * 2 + c
    t_cross = (1 - yl) * 2 + 1 - c
    t_far0 = (1 - yl) * 2
    t_far1 = (1 - yl) * 2 + 1
    p_flip = p + 1 - 2 * yh
    sibling = (p, t_sib)
    partner = (p, t_part)

    local = []

    def fetch(src, dst):
        copy = pltpu.make_async_copy(src, dst, lsem.at[len(local)])
        copy.start()
        local.append(copy)
        return copy

    own_video = fetch(video, vb.at[t])
    own_copies = [
        fetch(sk, kb.at[pl.ds(OWN_STALE, ROWS)]),
        fetch(sv, vvb.at[pl.ds(OWN_STALE, ROWS)]),
    ]
    text_copies = [fetch(tk, kb.at[pl.ds(0, TEXT)]), fetch(tv, vvb.at[pl.ds(0, TEXT)])]
    got_wq = fetch(wq, wqb)
    got_wk = fetch(wk, wkb)
    got_wv = fetch(wv, wvb)
    got_wo = fetch(wout.at[:, pl.ds(pl.multiple_of(t * FEAT, FEAT), FEAT)], wob.at[t])

    barrier = pltpu.get_barrier_semaphore()
    greeted = [sibling, (p, t_far0), (p, t_far1), (p_flip, t_far0), (p_flip, t_far1)]
    greeted += [(along_z(step), t) for step in Z_STEP.values()]
    greeted += [(along_x(*step), t) for step in X_STEP.values()]
    for device in greeted:
        pl.semaphore_signal(barrier, inc=1, device_id=device, device_id_type=pl.DeviceIdType.MESH)
    pl.semaphore_wait(barrier, len(greeted))

    sent = []

    def send(src, dst, recv, device):
        index = len(sent)

        def make():
            return pltpu.make_async_remote_copy(
                src_ref=src() if callable(src) else src, dst_ref=dst() if callable(dst) else dst,
                send_sem=ssem.at[index], recv_sem=rsem.at[recv],
                device_id=device, device_id_type=pl.DeviceIdType.MESH,
            )

        sent.append(make)
        make().start()

    def arrived(dst, recv):
        pltpu.make_async_copy(dst, dst, rsem.at[recv]).wait()

    for half, (r0, n) in enumerate(HALVES):
        send(video.at[pl.ds(r0, n)], vb.at[t, pl.ds(r0, n)], R_PART + half, partner)
    for half, (r0, n) in enumerate(HALVES):
        send(video.at[pl.ds(r0, n)], vb.at[t, pl.ds(r0, n)], R_SIB + half, sibling)

    def place_of(slot):
        return NEAR + (slot - 1) * ROWS if slot < 5 else FAR + (slot - 5) * ROWS

    def kv_slot(buffer, slot):
        return buffer.at[pl.ds(place_of(slot), ROWS)]

    def kv_arrived(slot):
        arrived(kv_slot(kb, slot), R_KV + 2 * slot)
        arrived(kv_slot(vvb, slot), R_KV + 2 * slot + 1)

    def kv_send(buffer, which, row, slot, device):
        src = buffer.at[pl.ds(pl.multiple_of(row, 16), ROWS)]
        send(src, kv_slot(buffer, slot), R_KV + 2 * slot + which, device)

    for which, own in enumerate((sk, sv)):
        buffer = (kb, vvb)[which]
        send(own, kv_slot(buffer, 1), R_KV + 2 + which, k1)
        send(own, kv_slot(buffer, 2), R_KV + 4 + which, k2)

    def spread(r, carry):
        posb[pl.ds(r, 1), :] = jnp.full((1, HEAD_DIM), pos[r], jnp.int32)
        return carry

    lax.fori_loop(0, ROWS, spread, 0)
    place = posb[...].astype(f32)
    frame = jnp.floor((place + 0.5) * (1.0 / 3600.0))
    within = place - 3600.0 * frame
    high = jnp.floor((within + 0.5) * (1.0 / 80.0))
    across = within - 80.0 * high
    lane = lax.broadcasted_iota(jnp.int32, (ROWS, HEAD_DIM), 1)
    angle = jnp.where(lane < 16, frame, jnp.where(lane < 72, high, across)) * rates[...]
    even = lane % 2 == 0
    cosb[...] = jnp.cos(angle)
    sine = jnp.sin(angle)
    sinb[...] = jnp.where(even, -sine, sine)
    stp[...] = jnp.zeros(stp.shape, f32)

    def normalise(r0, n):
        blocks = [vb[f, r0 : r0 + n, :].astype(f32) for f in range(4)]
        mean = sum(jnp.sum(b, axis=1, keepdims=True) for b in blocks) * (1.0 / D)
        spread = sum(jnp.sum((b - mean) ** 2, axis=1, keepdims=True) for b in blocks) * (1.0 / D)
        rstd = lax.rsqrt(spread + EPSILON)
        for f in range(4):
            cols = slice(f * FEAT, (f + 1) * FEAT)
            nb[r0 : r0 + n, cols] = (
                (blocks[f] - mean) * rstd * (1.0 + scale[:, cols]) + shift[:, cols]
            ).astype(bf16)

    def rows_of(slot, half):
        r0, n = HALVES[half]
        return vb.at[slot, pl.ds(r0, n)]

    own_video.wait()
    for copy in own_copies:
        copy.wait()
    for half in range(2):
        arrived(rows_of(t_part, half), R_PART + half)
        send(rows_of(t_part, half), rows_of(t_part, half), R_FWD + half, sibling)
        if half == 0:
            kv_arrived(1)
            kv_arrived(2)
            near_a = c * place_of(1) + (1 - c) * OWN_STALE
            near_b = c * place_of(2) + (1 - c) * OWN_STALE
            to_a = (c * k1[0] + (1 - c) * k3[0], t)
            to_b = (c * k2[0] + (1 - c) * k4[0], t)
            for which, buffer in enumerate((kb, vvb)):
                kv_send(buffer, which, near_a, 3, to_a)
                kv_send(buffer, which, near_b, 4, to_b)
    for half in range(2):
        arrived(rows_of(t_sib, half), R_SIB + half)
        arrived(rows_of(t_cross, half), R_FWD + half)
        normalise(*HALVES[half])

    def project(weight, gain, target):
        flat = jnp.dot(nb[...], weight[...], preferred_element_type=f32)
        for h in range(LOCAL_HEADS):
            hs = slice(h * HEAD_DIM, (h + 1) * HEAD_DIM)
            v = flat[:, hs]
            v = v * lax.rsqrt(jnp.mean(v * v, axis=1, keepdims=True) + EPSILON) * gain[...]
            other = jnp.where(even, pltpu.roll(v, HEAD_DIM - 1, 1), pltpu.roll(v, 1, 1))
            target[:, hs] = (v * cosb[...] + other * sinb[...]).astype(bf16)

    got_wq.wait()
    project(wqb, q_gain, qb.at[0])
    for slot, device in ((1, q1), (2, q2), (3, q3), (4, q4)):
        send(qb.at[0], qb.at[slot], R_Q + slot, device)

    kv_arrived(3)
    kv_arrived(4)
    far_a = c * place_of(3) + (1 - c) * place_of(4)
    to_v = (c * k4[0] + (1 - c) * k3[0], t)
    kv_send(kb, 0, far_a, 5, k1)
    kv_send(kb, 0, place_of(4), 6, k2)
    kv_send(vvb, 1, far_a, 5, k1)
    kv_send(vvb, 1, place_of(4), 6, k2)
    kv_send(kb, 0, far_a, 7, k3)
    kv_send(vvb, 1, place_of(4), 7, to_v)

    got_wk.wait()
    project(wkb, k_gain, kb.at[pl.ds(FRESH, ROWS)])
    got_wv.wait()
    vvb[FRESH : FRESH + ROWS, :] = jnp.dot(nb[...], wvb[...], preferred_element_type=f32).astype(bf16)
    out_k = fetch(kb.at[pl.ds(FRESH, ROWS)], fk)
    out_v = fetch(vvb.at[pl.ds(FRESH, ROWS)], fv)
    for copy in text_copies:
        copy.wait()

    def heads(h):
        return slice(h * HEAD_DIM, (h + 1) * HEAD_DIM)

    def tiles(array):
        return [
            array[:, i : min(i + HEAD_DIM, array.shape[1])] for i in range(0, array.shape[1], HEAD_DIM)
        ]

    def join(op, wide, tile):
        n = tile.shape[1]
        if n == HEAD_DIM:
            return op(wide, tile)
        return jnp.concatenate([op(wide[:, :n], tile), wide[:, n:]], axis=1)

    def row_top(scores):
        parts = tiles(scores)
        top = parts[0]
        for part in parts[1:]:
            top = join(jnp.maximum, top, part)
        return jnp.broadcast_to(jnp.max(top, axis=1, keepdims=True), (ROWS, HEAD_DIM))

    def weigh(scores, top, total):
        weights = [
            jnp.exp2((part - top[:, : part.shape[1]]) * EXP_FACTOR) for part in tiles(scores)
        ]
        for part in weights:
            total = join(jnp.add, total, part)
        return jnp.concatenate([part.astype(bf16) for part in weights], axis=1), total

    def scores_of(j, h, k0, n):
        return lax.dot_general(
            qb[j, :, heads(h)], kb[pl.ds(k0, n), heads(h)], (((1,), (1,)), ((), ())),
            preferred_element_type=f32,
        )

    def product(weights, h, k0, n):
        return jnp.dot(weights, vvb[pl.ds(k0, n), heads(h)], preferred_element_type=f32)

    live = lax.broadcasted_iota(jnp.int32, (1, TEXT), 1) < count[0]
    for h in range(LOCAL_HEADS):
        scores = jnp.where(live, scores_of(0, h, 0, TEXT), -1e30)
        top = row_top(scores)
        weights, total = weigh(scores, top, jnp.zeros((ROWS, HEAD_DIM), f32))
        ob[0, :, heads(h)] = product(weights, h, 0, TEXT)
        tops[0, h] = top
        sums[0, h] = total

    def q_arrived(slot):
        arrived(qb.at[slot], R_Q + slot)

    def half_step(j, k0, first):
        def score(h):
            scores = scores_of(j, h, k0, SPAN)
            sb[h % 2] = scores
            return row_top(scores)

        seen = score(0)
        for h in range(LOCAL_HEADS):
            before = jnp.where(first, -1e30, tops[j, h])
            top = jnp.maximum(before, seen)
            old = jnp.exp2((before - top) * EXP_FACTOR)
            if h + 1 < LOCAL_HEADS:
                seen = score(h + 1)
            weights, total = weigh(sb[h % 2], top, jnp.where(first, 0.0, sums[j, h]) * old)
            ob[j, :, heads(h)] = (
                jnp.where(first, 0.0, ob[j, :, heads(h)]) * old + product(weights, h, k0, SPAN)
            )
            tops[j, h] = top
            sums[j, h] = total

    column = lax.broadcasted_iota(jnp.int32, (ROWS, HEAD_DIM), 1)

    def pack(j):
        stats = jnp.zeros((ROWS, HEAD_DIM), f32)
        for h in range(LOCAL_HEADS):
            stats = jnp.where(column == h, tops[j, h], stats)
            stats = jnp.where(column == 3 + h, jnp.sum(sums[j, h], axis=1, keepdims=True), stats)
        stp[0:ROWS, :] = stats
        ss[j] = jnp.transpose(stp[...])[0:8, :]

    def give_back(j, device):
        return [
            pltpu.make_async_remote_copy(
                src_ref=source.at[j], dst_ref=target.at[j], send_sem=osem.at[2 * j + k],
                recv_sem=rsem.at[R_RS + 2 * j + k], device_id=device, device_id_type=pl.DeviceIdType.MESH,
            )
            for k, (source, target) in enumerate(((so, ro), (ss, rs)))
        ]

    far_q = (1 - c) * 3 + c * 4
    wo_recv = R_WO + t

    def step(i, codes):
        slots, parts, z_steps, x_steps, group = codes
        n = group * 8 + i
        j = slots % 8
        part = parts % 2

        for when, slot in ((1, 1), (2, 2), (7, 5), (9, 6), (11, 7)):
            pl.when(n == when)(functools.partial(q_arrived, slot))

        @pl.when(n == 3)
        def _():
            q_arrived(3)
            q_arrived(4)
            send(lambda: qb.at[far_q], lambda: qb.at[5], R_Q + 5, q1)
            send(lambda: qb.at[4], lambda: qb.at[6], R_Q + 6, q2)
            send(lambda: qb.at[far_q], lambda: qb.at[7], R_Q + 7, q3)

        @pl.when(n == 5)
        def _():
            for slot in (5, 6, 7):
                kv_arrived(slot)
            for user, device in ((t_sib, sibling), (t_far0, (p, t_far0)), (t_far1, (p_flip, t_far1))):
                send(
                    lambda user=user: wout.at[:, pl.ds(pl.multiple_of(user * FEAT, FEAT), FEAT)],
                    lambda: wob.at[t], wo_recv, device,
                )

        k0 = NEAR + part * (FAR - NEAR) - (n // 15) * ROWS
        half_step(j, pl.multiple_of(k0, 16), jnp.logical_and(part == 0, n > 0))

        @pl.when(part == 1)
        def _():
            pack(j)

        @pl.when(jnp.logical_and(part == 1, n < 15))
        def _():
            so[j] = ob[j].astype(bf16)
            shift_z = z_steps % 8 - 3
            shift_x = x_steps % 4 - 1
            flip = (x_steps // 4) % 2
            owner = (1 - c) * along_z(shift_z) + c * along_x(shift_x, flip)
            for copy in give_back(j, (owner, t)):
                copy.start()

        return slots // 8, parts // 2, z_steps // 8, x_steps // 8, group

    first_codes, later_codes = step_codes(0), step_codes(8)

    def eight(group, carry):
        codes = tuple(a + group * (b - a) for a, b in zip(first_codes, later_codes))
        lax.fori_loop(0, 8, step, codes + (group,))
        return carry

    lax.fori_loop(0, 2, eight, 0)

    for slot in range(1, 8):
        arrived(ro.at[slot], R_RS + 2 * slot)
        arrived(rs.at[slot], R_RS + 2 * slot + 1)
    stats = [ss[0]] + [rs[slot] for slot in range(1, 8)]
    top = stats[0][0:3]
    for part in stats[1:]:
        top = jnp.maximum(top, part[0:3])
    shares = [jnp.exp2((part[0:3] - top) * EXP_FACTOR) for part in stats]
    total = sum(share * part[3:6] for share, part in zip(shares, stats))
    blank = jnp.zeros((5, 384), f32)
    rows = [jnp.concatenate([share / total, blank], axis=0) for share in shares]
    rows.append(jnp.zeros((64, 384), f32))
    weight = jnp.transpose(jnp.concatenate(rows, axis=0))[0:ROWS]
    for h in range(LOCAL_HEADS):
        summed = ob[0, :, heads(h)] * weight[:, h : h + 1]
        for slot in range(1, 8):
            summed += ro[slot, :, heads(h)].astype(f32) * weight[:, 8 * slot + h : 8 * slot + h + 1]
        atb[t, :, heads(h)] = summed.astype(bf16)

    send(atb.at[t], atb.at[t], R_ATT + 1, partner)
    send(atb.at[t], atb.at[t], R_ATT, sibling)
    got_wo.wait()
    for slot in (t_sib, t_far0, t_far1):
        arrived(wob.at[slot], R_WO + slot)

    def term(slot):
        return jnp.dot(atb[slot], wob[slot], preferred_element_type=f32)

    branch = term(t)
    arrived(atb.at[t_sib], R_ATT)
    branch = branch + term(t_sib)
    arrived(atb.at[t_part], R_ATT + 1)
    send(atb.at[t_part], atb.at[t_part], R_ATT + 2, sibling)
    branch = branch + term(t_part)
    arrived(atb.at[t_cross], R_ATT + 2)
    branch = branch + term(t_cross)
    mixed[...] = vb[t].astype(f32) + gate[...][None, :] * branch

    out_k.wait()
    out_v.wait()
    for make in sent:
        make().wait_send()
    for slot in range(1, 8):
        for copy in give_back(slot, (p, t_sib)):
            copy.wait_send()


def hand_over(*refs):
    sources, targets, held, sems = refs[:3], refs[3:6], refs[6:9], refs[9]
    inward = [pltpu.make_async_copy(a, b, sems.at[i]) for i, (a, b) in enumerate(zip(sources, held))]
    outward = [
        pltpu.make_async_copy(a, b, sems.at[3 + i]) for i, (a, b) in enumerate(zip(held, targets))
    ]
    for copy in inward:
        copy.start()
    for first, second in zip(inward, outward):
        first.wait()
        second.start()
    for copy in outward:
        copy.wait()


def shards(
    video, positions, text_count, mod_shift, mod_scale, gate, w_query, w_key, w_value, w_out,
    q_gain, k_gain, stale_keys, stale_values, text_keys, text_values,
):
    bf16, f32 = jnp.bfloat16, jnp.float32
    vmem = pl.BlockSpec(memory_space=pltpu.VMEM)
    smem = pl.BlockSpec(memory_space=pltpu.SMEM)
    hbm = pl.BlockSpec(memory_space=pl.ANY)
    outs = (
        jax.ShapeDtypeStruct((ROWS, FEAT), f32),
        jax.ShapeDtypeStruct((ROWS, WIDTH), bf16),
        jax.ShapeDtypeStruct((ROWS, WIDTH), bf16),
    )
    made = pl.pallas_call(
        kernel,
        out_shape=outs,
        in_specs=[
            hbm, smem, smem, vmem, vmem, vmem, hbm, hbm, hbm, hbm, vmem, vmem, hbm, hbm, hbm, hbm,
            vmem,
        ],
        out_specs=(vmem, hbm, hbm),
        scratch_shapes=[
            pltpu.VMEM((4, ROWS, FEAT), bf16),
            pltpu.VMEM((ROWS, D), bf16),
            pltpu.VMEM((D, WIDTH), bf16),
            pltpu.VMEM((D, WIDTH), bf16),
            pltpu.VMEM((D, WIDTH), bf16),
            pltpu.VMEM((KEYS, WIDTH), bf16),
            pltpu.VMEM((KEYS, WIDTH), bf16),
            pltpu.VMEM((8, ROWS, WIDTH), bf16),
            pltpu.VMEM((ROWS, HEAD_DIM), jnp.int32),
            pltpu.VMEM((ROWS, HEAD_DIM), f32),
            pltpu.VMEM((ROWS, HEAD_DIM), f32),
            pltpu.VMEM((2, ROWS, SPAN), f32),
            pltpu.VMEM((8, ROWS, WIDTH), f32),
            pltpu.VMEM((8, LOCAL_HEADS, ROWS, HEAD_DIM), f32),
            pltpu.VMEM((8, LOCAL_HEADS, ROWS, HEAD_DIM), f32),
            pltpu.VMEM((384, HEAD_DIM), f32),
            pltpu.VMEM((8, ROWS, WIDTH), bf16),
            pltpu.VMEM((8, 8, 384), f32),
            pltpu.VMEM((8, ROWS, WIDTH), bf16),
            pltpu.VMEM((8, 8, 384), f32),
            pltpu.VMEM((4, WIDTH, FEAT), bf16),
            pltpu.VMEM((4, ROWS, WIDTH), bf16),
            pltpu.SemaphoreType.DMA((N_SEND,)),
            pltpu.SemaphoreType.DMA((16,)),
            pltpu.SemaphoreType.DMA((N_RECV,)),
            pltpu.SemaphoreType.DMA((N_LOCAL,)),
        ],
        compiler_params=pltpu.CompilerParams(
            collective_id=0, has_side_effects=True, vmem_limit_bytes=60 * 1024 * 1024
        ),
        name="attention_half",
    )(
        video,
        positions,
        text_count,
        mod_shift.reshape(1, D),
        mod_scale.reshape(1, D),
        gate,
        w_query,
        w_key,
        w_value,
        w_out,
        q_gain.reshape(1, HEAD_DIM),
        k_gain.reshape(1, HEAD_DIM),
        stale_keys,
        stale_values,
        text_keys,
        text_values,
        jnp.asarray(pair_rates()),
    )
    return pl.pallas_call(
        hand_over,
        out_shape=outs,
        in_specs=[hbm] * 3,
        out_specs=(hbm,) * 3,
        scratch_shapes=[pltpu.VMEM(out.shape, out.dtype) for out in outs]
        + [pltpu.SemaphoreType.DMA((6,))],
        compiler_params=pltpu.CompilerParams(vmem_limit_bytes=60 * 1024 * 1024),
        name="hand_over",
    )(*made)


def solution(mesh):
    return jax.shard_map(
        shards,
        mesh=mesh,
        in_specs=(
            P("patch", "tensor"),
            P("patch"),
            P(),
            P(),
            P(),
            P("tensor"),
            P(None, "tensor"),
            P(None, "tensor"),
            P(None, "tensor"),
            P("tensor", None),
            P(),
            P(),
            P("patch", "tensor"),
            P("patch", "tensor"),
            P(None, "tensor"),
            P(None, "tensor"),
        ),
        out_specs=(P("patch", "tensor"), P("patch", "tensor"), P("patch", "tensor")),
        check_vma=False,
    )
```

```python
import functools
import math

import jax
import jax.numpy as jnp
import numpy as np
from jax import lax
from jax.experimental import pallas as pl
from jax.experimental.pallas import tpu as pltpu
from jax.sharding import PartitionSpec as P

D = 3072
HEAD_DIM = 128
LOCAL_HEADS = 3
ROWS = 272
WIDTH = LOCAL_HEADS * HEAD_DIM
FEAT = 768
TEXT = 256
EPSILON = 1e-06
EXP_FACTOR = math.log2(math.e) / math.sqrt(HEAD_DIM)

NEAR = TEXT
FRESH = NEAR + 4 * ROWS
FAR = FRESH + ROWS
OWN_STALE = FAR + 3 * ROWS
KEYS = OWN_STALE + ROWS
SPAN = 4 * ROWS

HALVES = ((0, 144), (144, 128))

STEPS = (
    (0, 0), (1, 0), (2, 0), (3, 0), (4, 0), (1, 1), (2, 1), (3, 1),
    (4, 1), (5, 0), (5, 1), (6, 0), (6, 1), (7, 0), (7, 1), (0, 1),
)
Z_STEP = {1: -1, 2: 1, 3: -2, 4: 2, 5: -3, 6: 3, 7: 4}
X_STEP = {1: (-1, 0), 2: (1, 0), 3: (2, 0), 4: (0, 1), 5: (-1, 1), 6: (1, 1), 7: (2, 1)}


def digits(values, base):
    total = 0
    for value in reversed(values):
        total = total * base + value
    return total


def step_codes(first):
    part = STEPS[first : first + 8]
    return (
        digits([slot for slot, _ in part], 8),
        digits([half for _, half in part], 2),
        digits([Z_STEP.get(slot, 0) + 3 for slot, _ in part], 8),
        digits([X_STEP.get(slot, (0, 0))[0] + 1 + 4 * X_STEP.get(slot, (0, 0))[1] for slot, _ in part], 8),
    )


R_SIB, R_PART, R_FWD, R_KV, R_Q, R_WO, R_RS, R_ATT = 0, 2, 4, 6, 22, 31, 35, 51
N_RECV = 54
N_SEND = 64
N_LOCAL = 16


def pair_rates():
    pairs = HEAD_DIM // 2
    frame = HEAD_DIM // 16
    high = (pairs - frame) // 2
    wide = pairs - frame - high
    rates = np.concatenate(
        [256.0 ** (-np.arange(n, dtype=np.float64) / n) for n in (frame, high, wide)]
    )
    return np.repeat(rates, 2).astype(np.float32)[None, :]


def kernel(
    video, pos, count, shift, scale, gate, wq, wk, wv, wout, q_gain, k_gain, sk, sv, tk, tv, rates,
    mixed, fk, fv,
    vb, nb, wqb, wkv, kb, vvb, qb, posb, cosb, sinb, sb, ob, tops, sums, stp, so, ss, ro, rs, wob, atb,
    ssem, osem, rsem, lsem,
):
    f32 = jnp.float32
    bf16 = jnp.bfloat16
    p = lax.axis_index("patch")
    t = lax.axis_index("tensor")
    x = p // 16
    z = (p // 2) % 8
    yh = p % 2
    yl = t // 2
    c = t % 2

    def along_z(step):
        return x * 16 + ((z + step + 8) % 8) * 2 + yh

    def along_x(step, flip):
        return ((x + step + 4) % 4) * 16 + z * 2 + yh + flip * (1 - 2 * yh)

    on_z = (along_z(1), along_z(-1), along_z(2), along_z(-2))
    on_x = (along_x(1, 0), along_x(-1, 0), along_x(2, 0), along_x(0, 1))
    k1, k2, k3, k4 = ((c * a + (1 - c) * b, t) for a, b in zip(on_z, on_x))
    q1, q2, q3, q4 = ((c * b + (1 - c) * a, t) for a, b in zip(on_z, on_x))
    t_sib = yl * 2 + 1 - c
    t_part = (1 - yl) * 2 + c
    t_cross = (1 - yl) * 2 + 1 - c
    t_far0 = (1 - yl) * 2
    t_far1 = (1 - yl) * 2 + 1
    p_flip = p + 1 - 2 * yh
    sibling = (p, t_sib)
    partner = (p, t_part)

    barrier = pltpu.get_barrier_semaphore()
    greeted = [sibling, (p, t_far0), (p, t_far1), (p_flip, t_far0), (p_flip, t_far1)]
    greeted += [(along_z(step), t) for step in Z_STEP.values()]
    greeted += [(along_x(*step), t) for step in X_STEP.values()]
    for device in greeted:
        pl.semaphore_signal(barrier, inc=1, device_id=device, device_id_type=pl.DeviceIdType.MESH)

    local = []

    def fetch(src, dst):
        copy = pltpu.make_async_copy(src, dst, lsem.at[len(local)])
        copy.start()
        local.append(copy)
        return copy

    own_video = fetch(video, vb.at[t])
    own_copies = [
        fetch(sk, kb.at[pl.ds(OWN_STALE, ROWS)]),
        fetch(sv, vvb.at[pl.ds(OWN_STALE, ROWS)]),
    ]
    text_copies = [fetch(tk, kb.at[pl.ds(0, TEXT)]), fetch(tv, vvb.at[pl.ds(0, TEXT)])]
    got_wq = fetch(wq, wqb)
    got_wk = fetch(wk, wkv.at[:, pl.ds(0, WIDTH)])
    got_wv = fetch(wv, wkv.at[:, pl.ds(WIDTH, WIDTH)])
    got_wo = fetch(wout.at[:, pl.ds(pl.multiple_of(t * FEAT, FEAT), FEAT)], wob.at[t])

    def spread(r, carry):
        posb[pl.ds(r, 1), :] = jnp.full((1, HEAD_DIM), pos[r], jnp.int32)
        return carry

    lax.fori_loop(0, ROWS, spread, 0)
    place = posb[...].astype(f32)
    frame = jnp.floor((place + 0.5) * (1.0 / 3600.0))
    within = place - 3600.0 * frame
    high = jnp.floor((within + 0.5) * (1.0 / 80.0))
    across = within - 80.0 * high
    lane = lax.broadcasted_iota(jnp.int32, (ROWS, HEAD_DIM), 1)
    angle = jnp.where(lane < 16, frame, jnp.where(lane < 72, high, across)) * rates[...]
    even = lane % 2 == 0
    cosb[...] = jnp.cos(angle)
    sine = jnp.sin(angle)
    sinb[...] = jnp.where(even, -sine, sine)
    stp[...] = jnp.zeros(stp.shape, f32)

    pl.semaphore_wait(barrier, len(greeted))

    sent = []

    def send(src, dst, recv, device):
        index = len(sent)

        def make():
            return pltpu.make_async_remote_copy(
                src_ref=src() if callable(src) else src, dst_ref=dst() if callable(dst) else dst,
                send_sem=ssem.at[index], recv_sem=rsem.at[recv],
                device_id=device, device_id_type=pl.DeviceIdType.MESH,
            )

        sent.append(make)
        make().start()

    def arrived(dst, recv):
        pltpu.make_async_copy(dst, dst, rsem.at[recv]).wait()

    for half, (r0, n) in enumerate(HALVES):
        send(video.at[pl.ds(r0, n)], vb.at[t, pl.ds(r0, n)], R_PART + half, partner)
    for half, (r0, n) in enumerate(HALVES):
        send(video.at[pl.ds(r0, n)], vb.at[t, pl.ds(r0, n)], R_SIB + half, sibling)

    def place_of(slot):
        return NEAR + (slot - 1) * ROWS if slot < 5 else FAR + (slot - 5) * ROWS

    def kv_slot(buffer, slot):
        return buffer.at[pl.ds(place_of(slot), ROWS)]

    def kv_arrived(slot):
        arrived(kv_slot(kb, slot), R_KV + 2 * slot)
        arrived(kv_slot(vvb, slot), R_KV + 2 * slot + 1)

    def kv_send(buffer, which, row, slot, device):
        src = buffer.at[pl.ds(pl.multiple_of(row, 16), ROWS)]
        send(src, kv_slot(buffer, slot), R_KV + 2 * slot + which, device)

    for which, own in enumerate((sk, sv)):
        buffer = (kb, vvb)[which]
        send(own, kv_slot(buffer, 1), R_KV + 2 + which, k1)
        send(own, kv_slot(buffer, 2), R_KV + 4 + which, k2)

    def normalise(r0, n):
        blocks = [vb[f, r0 : r0 + n, :].astype(f32) for f in range(4)]
        mean = sum(jnp.sum(b, axis=1, keepdims=True) for b in blocks) * (1.0 / D)
        spread = sum(jnp.sum((b - mean) ** 2, axis=1, keepdims=True) for b in blocks) * (1.0 / D)
        rstd = lax.rsqrt(spread + EPSILON)
        for f in range(4):
            cols = slice(f * FEAT, (f + 1) * FEAT)
            nb[r0 : r0 + n, cols] = (
                (blocks[f] - mean) * rstd * (1.0 + scale[:, cols]) + shift[:, cols]
            ).astype(bf16)

    def rows_of(slot, half):
        r0, n = HALVES[half]
        return vb.at[slot, pl.ds(r0, n)]

    far_a = c * place_of(3) + (1 - c) * place_of(4)
    near_a = c * place_of(1) + (1 - c) * OWN_STALE
    near_b = c * place_of(2) + (1 - c) * OWN_STALE
    to_a = (c * k1[0] + (1 - c) * k3[0], t)
    to_b = (c * k2[0] + (1 - c) * k4[0], t)

    def second_round(which):
        buffer = (kb, vvb)[which]
        for slot in (1, 2):
            arrived(kv_slot(buffer, slot), R_KV + 2 * slot + which)
        kv_send(buffer, which, near_a, 3, to_a)
        kv_send(buffer, which, near_b, 4, to_b)

    def third_round(which):
        buffer = (kb, vvb)[which]
        for slot in (3, 4):
            arrived(kv_slot(buffer, slot), R_KV + 2 * slot + which)
        kv_send(buffer, which, far_a, 5, k1)
        kv_send(buffer, which, place_of(4), 6, k2)
        if which == 0:
            kv_send(buffer, which, far_a, 7, k3)
        else:
            kv_send(buffer, which, place_of(4), 7, (c * k4[0] + (1 - c) * k3[0], t))

    def pass_features(half):
        arrived(rows_of(t_part, half), R_PART + half)
        send(rows_of(t_part, half), rows_of(t_part, half), R_FWD + half, sibling)

    def normalise_half(half):
        arrived(rows_of(t_sib, half), R_SIB + half)
        arrived(rows_of(t_cross, half), R_FWD + half)
        normalise(*HALVES[half])

    own_video.wait()
    for copy in own_copies:
        copy.wait()
    second_round(0)
    pass_features(0)
    second_round(1)
    third_round(0)
    pass_features(1)
    normalise_half(0)
    third_round(1)
    normalise_half(1)

    def turned(flat, gain, target):
        for h in range(LOCAL_HEADS):
            hs = slice(h * HEAD_DIM, (h + 1) * HEAD_DIM)
            v = flat[:, hs]
            v = v * lax.rsqrt(jnp.mean(v * v, axis=1, keepdims=True) + EPSILON) * gain[...]
            other = jnp.where(even, pltpu.roll(v, HEAD_DIM - 1, 1), pltpu.roll(v, 1, 1))
            target[:, hs] = (v * cosb[...] + other * sinb[...]).astype(bf16)

    got_wq.wait()
    turned(jnp.dot(nb[...], wqb[...], preferred_element_type=f32), q_gain, qb.at[0])
    for slot, device in ((1, q1), (2, q2), (3, q3), (4, q4)):
        send(qb.at[0], qb.at[slot], R_Q + slot, device)

    got_wk.wait()
    got_wv.wait()
    flat = jnp.dot(nb[...], wkv[...], preferred_element_type=f32)
    turned(flat[:, 0:WIDTH], k_gain, kb.at[pl.ds(FRESH, ROWS)])
    vvb[FRESH : FRESH + ROWS, :] = flat[:, WIDTH:].astype(bf16)
    out_k = fetch(kb.at[pl.ds(FRESH, ROWS)], fk)
    out_v = fetch(vvb.at[pl.ds(FRESH, ROWS)], fv)
    for copy in text_copies:
        copy.wait()

    def heads(h):
        return slice(h * HEAD_DIM, (h + 1) * HEAD_DIM)

    def tiles(array):
        return [
            array[:, i : min(i + HEAD_DIM, array.shape[1])] for i in range(0, array.shape[1], HEAD_DIM)
        ]

    def join(op, wide, tile):
        n = tile.shape[1]
        if n == HEAD_DIM:
            return op(wide, tile)
        return jnp.concatenate([op(wide[:, :n], tile), wide[:, n:]], axis=1)

    def row_top(scores):
        parts = tiles(scores)
        top = parts[0]
        for part in parts[1:]:
            top = join(jnp.maximum, top, part)
        return jnp.broadcast_to(jnp.max(top, axis=1, keepdims=True), (ROWS, HEAD_DIM))

    def weigh(scores, top, total):
        weights = [
            jnp.exp2((part - top[:, : part.shape[1]]) * EXP_FACTOR) for part in tiles(scores)
        ]
        for part in weights:
            total = join(jnp.add, total, part)
        return jnp.concatenate([part.astype(bf16) for part in weights], axis=1), total

    def scores_of(j, h, k0, n):
        return lax.dot_general(
            qb[j, :, heads(h)], kb[pl.ds(k0, n), heads(h)], (((1,), (1,)), ((), ())),
            preferred_element_type=f32,
        )

    def product(weights, h, k0, n):
        return jnp.dot(weights, vvb[pl.ds(k0, n), heads(h)], preferred_element_type=f32)

    live = lax.broadcasted_iota(jnp.int32, (1, TEXT), 1) < count[0]
    for h in range(LOCAL_HEADS):
        scores = jnp.where(live, scores_of(0, h, 0, TEXT), -1e30)
        top = row_top(scores)
        weights, total = weigh(scores, top, jnp.zeros((ROWS, HEAD_DIM), f32))
        ob[0, :, heads(h)] = product(weights, h, 0, TEXT)
        tops[0, h] = top
        sums[0, h] = total

    def q_arrived(slot):
        arrived(qb.at[slot], R_Q + slot)

    def half_step(j, k0, first):
        def score(h):
            scores = scores_of(j, h, k0, SPAN)
            sb[h % 2] = scores
            return row_top(scores)

        seen = score(0)
        for h in range(LOCAL_HEADS):
            before = jnp.where(first, -1e30, tops[j, h])
            top = jnp.maximum(before, seen)
            old = jnp.exp2((before - top) * EXP_FACTOR)
            if h + 1 < LOCAL_HEADS:
                seen = score(h + 1)
            weights, total = weigh(sb[h % 2], top, jnp.where(first, 0.0, sums[j, h]) * old)
            ob[j, :, heads(h)] = (
                jnp.where(first, 0.0, ob[j, :, heads(h)]) * old + product(weights, h, k0, SPAN)
            )
            tops[j, h] = top
            sums[j, h] = total

    column = lax.broadcasted_iota(jnp.int32, (ROWS, HEAD_DIM), 1)

    def pack(j):
        stats = jnp.zeros((ROWS, HEAD_DIM), f32)
        for h in range(LOCAL_HEADS):
            stats = jnp.where(column == h, tops[j, h], stats)
            stats = jnp.where(column == 3 + h, jnp.sum(sums[j, h], axis=1, keepdims=True), stats)
        stp[0:ROWS, :] = stats
        ss[j] = jnp.transpose(stp[...])[0:8, :]

    def give_back(j, device):
        return [
            pltpu.make_async_remote_copy(
                src_ref=source.at[j], dst_ref=target.at[j], send_sem=osem.at[2 * j + k],
                recv_sem=rsem.at[R_RS + 2 * j + k], device_id=device, device_id_type=pl.DeviceIdType.MESH,
            )
            for k, (source, target) in enumerate(((so, ro), (ss, rs)))
        ]

    far_q = (1 - c) * 3 + c * 4
    wo_recv = R_WO + t
    q_last = ((1 - c) * q4[0] + c * q3[0], t)

    def step(i, codes):
        slots, parts, z_steps, x_steps, group = codes
        n = group * 8 + i
        j = slots % 8
        part = parts % 2

        for when, slot in ((1, 1), (2, 2), (9, 5), (11, 6)):
            pl.when(n == when)(functools.partial(q_arrived, slot))

        @pl.when(n == 3)
        def _():
            q_arrived(3)
            q_arrived(4)
            send(lambda: qb.at[far_q], lambda: qb.at[5], R_Q + 5, q1)
            send(lambda: qb.at[4], lambda: qb.at[6], R_Q + 6, q2)
            for half, (source, device) in enumerate(((far_q, q3), (4, q_last))):
                r0, rows = HALVES[half]
                send(
                    lambda source=source, r0=r0, rows=rows: qb.at[source, pl.ds(r0, rows)],
                    lambda r0=r0, rows=rows: qb.at[7, pl.ds(r0, rows)], R_Q + 7 + half, device,
                )

        @pl.when(n == 13)
        def _():
            for half, (r0, rows) in enumerate(HALVES):
                arrived(qb.at[7, pl.ds(r0, rows)], R_Q + 7 + half)

        @pl.when(n == 5)
        def _():
            for slot in (5, 6, 7):
                kv_arrived(slot)
            for user, device in ((t_sib, sibling), (t_far0, (p, t_far0)), (t_far1, (p_flip, t_far1))):
                send(
                    lambda user=user: wout.at[:, pl.ds(pl.multiple_of(user * FEAT, FEAT), FEAT)],
                    lambda: wob.at[t], wo_recv, device,
                )

        k0 = NEAR + part * (FAR - NEAR) - (n // 15) * ROWS
        half_step(j, pl.multiple_of(k0, 16), jnp.logical_and(part == 0, n > 0))

        @pl.when(part == 1)
        def _():
            pack(j)

        @pl.when(jnp.logical_and(part == 1, n < 15))
        def _():
            so[j] = ob[j].astype(bf16)
            shift_z = z_steps % 8 - 3
            shift_x = x_steps % 4 - 1
            flip = (x_steps // 4) % 2
            owner = (1 - c) * along_z(shift_z) + c * along_x(shift_x, flip)
            for copy in give_back(j, (owner, t)):
                copy.start()

        return slots // 8, parts // 2, z_steps // 8, x_steps // 8, group

    first_codes, later_codes = step_codes(0), step_codes(8)

    def eight(group, carry):
        codes = tuple(a + group * (b - a) for a, b in zip(first_codes, later_codes))
        lax.fori_loop(0, 8, step, codes + (group,))
        return carry

    lax.fori_loop(0, 2, eight, 0)

    for slot in range(1, 8):
        arrived(ro.at[slot], R_RS + 2 * slot)
        arrived(rs.at[slot], R_RS + 2 * slot + 1)
    stats = [ss[0]] + [rs[slot] for slot in range(1, 8)]
    top = stats[0][0:3]
    for part in stats[1:]:
        top = jnp.maximum(top, part[0:3])
    shares = [jnp.exp2((part[0:3] - top) * EXP_FACTOR) for part in stats]
    total = sum(share * part[3:6] for share, part in zip(shares, stats))
    blank = jnp.zeros((5, 384), f32)
    rows = [jnp.concatenate([share / total, blank], axis=0) for share in shares]
    rows.append(jnp.zeros((64, 384), f32))
    weight = jnp.transpose(jnp.concatenate(rows, axis=0))[0:ROWS]
    for h in range(LOCAL_HEADS):
        summed = ob[0, :, heads(h)] * weight[:, h : h + 1]
        for slot in range(1, 8):
            summed += ro[slot, :, heads(h)].astype(f32) * weight[:, 8 * slot + h : 8 * slot + h + 1]
        atb[t, :, heads(h)] = summed.astype(bf16)

    send(atb.at[t], atb.at[t], R_ATT + 1, partner)
    send(atb.at[t], atb.at[t], R_ATT, sibling)
    got_wo.wait()
    for slot in (t_sib, t_far0, t_far1):
        arrived(wob.at[slot], R_WO + slot)

    def term(slot):
        return jnp.dot(atb[slot], wob[slot], preferred_element_type=f32)

    branch = term(t)
    arrived(atb.at[t_sib], R_ATT)
    branch = branch + term(t_sib)
    arrived(atb.at[t_part], R_ATT + 1)
    send(atb.at[t_part], atb.at[t_part], R_ATT + 2, sibling)
    branch = branch + term(t_part)
    arrived(atb.at[t_cross], R_ATT + 2)
    branch = branch + term(t_cross)
    mixed[...] = vb[t].astype(f32) + gate[...][None, :] * branch

    out_k.wait()
    out_v.wait()
    for make in sent:
        make().wait_send()
    for slot in range(1, 8):
        for copy in give_back(slot, (p, t_sib)):
            copy.wait_send()


def hand_over(*refs):
    sources, targets, held, sems = refs[:3], refs[3:6], refs[6:9], refs[9]
    inward = [pltpu.make_async_copy(a, b, sems.at[i]) for i, (a, b) in enumerate(zip(sources, held))]
    outward = [
        pltpu.make_async_copy(a, b, sems.at[3 + i]) for i, (a, b) in enumerate(zip(held, targets))
    ]
    for copy in inward:
        copy.start()
    for first, second in zip(inward, outward):
        first.wait()
        second.start()
    for copy in outward:
        copy.wait()


def shards(
    video, positions, text_count, mod_shift, mod_scale, gate, w_query, w_key, w_value, w_out,
    q_gain, k_gain, stale_keys, stale_values, text_keys, text_values,
):
    bf16, f32 = jnp.bfloat16, jnp.float32
    vmem = pl.BlockSpec(memory_space=pltpu.VMEM)
    smem = pl.BlockSpec(memory_space=pltpu.SMEM)
    hbm = pl.BlockSpec(memory_space=pl.ANY)
    outs = (
        jax.ShapeDtypeStruct((ROWS, FEAT), f32),
        jax.ShapeDtypeStruct((ROWS, WIDTH), bf16),
        jax.ShapeDtypeStruct((ROWS, WIDTH), bf16),
    )
    made = pl.pallas_call(
        kernel,
        out_shape=outs,
        in_specs=[
            hbm, smem, smem, vmem, vmem, vmem, hbm, hbm, hbm, hbm, vmem, vmem, hbm, hbm, hbm, hbm,
            vmem,
        ],
        out_specs=(vmem, hbm, hbm),
        scratch_shapes=[
            pltpu.VMEM((4, ROWS, FEAT), bf16),
            pltpu.VMEM((ROWS, D), bf16),
            pltpu.VMEM((D, WIDTH), bf16),
            pltpu.VMEM((D, 2 * WIDTH), bf16),
            pltpu.VMEM((KEYS, WIDTH), bf16),
            pltpu.VMEM((KEYS, WIDTH), bf16),
            pltpu.VMEM((8, ROWS, WIDTH), bf16),
            pltpu.VMEM((ROWS, HEAD_DIM), jnp.int32),
            pltpu.VMEM((ROWS, HEAD_DIM), f32),
            pltpu.VMEM((ROWS, HEAD_DIM), f32),
            pltpu.VMEM((2, ROWS, SPAN), f32),
            pltpu.VMEM((8, ROWS, WIDTH), f32),
            pltpu.VMEM((8, LOCAL_HEADS, ROWS, HEAD_DIM), f32),
            pltpu.VMEM((8, LOCAL_HEADS, ROWS, HEAD_DIM), f32),
            pltpu.VMEM((384, HEAD_DIM), f32),
            pltpu.VMEM((8, ROWS, WIDTH), bf16),
            pltpu.VMEM((8, 8, 384), f32),
            pltpu.VMEM((8, ROWS, WIDTH), bf16),
            pltpu.VMEM((8, 8, 384), f32),
            pltpu.VMEM((4, WIDTH, FEAT), bf16),
            pltpu.VMEM((4, ROWS, WIDTH), bf16),
            pltpu.SemaphoreType.DMA((N_SEND,)),
            pltpu.SemaphoreType.DMA((16,)),
            pltpu.SemaphoreType.DMA((N_RECV,)),
            pltpu.SemaphoreType.DMA((N_LOCAL,)),
        ],
        compiler_params=pltpu.CompilerParams(
            collective_id=0, has_side_effects=True, vmem_limit_bytes=60 * 1024 * 1024
        ),
        name="attention_half",
    )(
        video,
        positions,
        text_count,
        mod_shift.reshape(1, D),
        mod_scale.reshape(1, D),
        gate,
        w_query,
        w_key,
        w_value,
        w_out,
        q_gain.reshape(1, HEAD_DIM),
        k_gain.reshape(1, HEAD_DIM),
        stale_keys,
        stale_values,
        text_keys,
        text_values,
        jnp.asarray(pair_rates()),
    )
    return pl.pallas_call(
        hand_over,
        out_shape=outs,
        in_specs=[hbm] * 3,
        out_specs=(hbm,) * 3,
        scratch_shapes=[pltpu.VMEM(out.shape, out.dtype) for out in outs]
        + [pltpu.SemaphoreType.DMA((6,))],
        compiler_params=pltpu.CompilerParams(vmem_limit_bytes=60 * 1024 * 1024),
        name="hand_over",
    )(*made)


def solution(mesh):
    return jax.shard_map(
        shards,
        mesh=mesh,
        in_specs=(
            P("patch", "tensor"),
            P("patch"),
            P(),
            P(),
            P(),
            P("tensor"),
            P(None, "tensor"),
            P(None, "tensor"),
            P(None, "tensor"),
            P("tensor", None),
            P(),
            P(),
            P("patch", "tensor"),
            P("patch", "tensor"),
            P(None, "tensor"),
            P(None, "tensor"),
        ),
        out_specs=(P("patch", "tensor"), P("patch", "tensor"), P("patch", "tensor")),
        check_vma=False,
    )
```

```python
import functools
import math

import jax
import jax.numpy as jnp
import numpy as np
from jax import lax
from jax.experimental import pallas as pl
from jax.experimental.pallas import tpu as pltpu
from jax.sharding import PartitionSpec as P

D = 3072
HEAD_DIM = 128
LOCAL_HEADS = 3
ROWS = 272
WIDTH = LOCAL_HEADS * HEAD_DIM
FEAT = 768
TEXT = 256
EPSILON = 1e-06
EXP_FACTOR = math.log2(math.e) / math.sqrt(HEAD_DIM)

FRESH = TEXT
NEAR = FRESH + ROWS
OWN_STALE = NEAR + 4 * ROWS
FAR = OWN_STALE + ROWS
KEYS = FAR + 3 * ROWS
FIRST_SPAN = 5 * ROWS
LATER_SPAN = 3 * ROWS

HALVES = ((0, 144), (144, 128))

STEPS = (
    (0, 0), (1, 0), (2, 0), (3, 0), (4, 0), (1, 1), (2, 1), (3, 1),
    (4, 1), (5, 0), (5, 1), (6, 0), (6, 1), (7, 0), (7, 1), (0, 1),
)
Z_STEP = {1: -1, 2: 1, 3: -2, 4: 2, 5: -3, 6: 3, 7: 4}
X_STEP = {1: (-1, 0), 2: (1, 0), 3: (2, 0), 4: (0, 1), 5: (-1, 1), 6: (1, 1), 7: (2, 1)}


def digits(values, base):
    total = 0
    for value in reversed(values):
        total = total * base + value
    return total


def step_codes(first):
    part = STEPS[first : first + 8]
    return (
        digits([slot for slot, _ in part], 8),
        digits([half for _, half in part], 2),
        digits([Z_STEP.get(slot, 0) + 3 for slot, _ in part], 8),
        digits([X_STEP.get(slot, (0, 0))[0] + 1 + 4 * X_STEP.get(slot, (0, 0))[1] for slot, _ in part], 8),
    )


R_SIB, R_PART, R_FWD, R_KV, R_Q, R_WO, R_RS, R_ATT = 0, 2, 4, 6, 22, 31, 35, 51
N_RECV = 54
N_SEND = 64
N_LOCAL = 16


def pair_rates():
    pairs = HEAD_DIM // 2
    frame = HEAD_DIM // 16
    high = (pairs - frame) // 2
    wide = pairs - frame - high
    rates = np.concatenate(
        [256.0 ** (-np.arange(n, dtype=np.float64) / n) for n in (frame, high, wide)]
    )
    return np.repeat(rates, 2).astype(np.float32)[None, :]


def kernel(
    video, pos, count, shift, scale, gate, wq, wk, wv, wout, q_gain, k_gain, sk, sv, tk, tv, rates,
    mixed, fk, fv,
    vb, nb, wqb, wkv, kb, vvb, qb, posb, cosb, sinb, sb, ob, tops, sums, stp, so, ss, ro, rs, wob, atb,
    ssem, osem, rsem, lsem,
):
    f32 = jnp.float32
    bf16 = jnp.bfloat16
    p = lax.axis_index("patch")
    t = lax.axis_index("tensor")
    x = p // 16
    z = (p // 2) % 8
    yh = p % 2
    yl = t // 2
    c = t % 2

    def along_z(step):
        return x * 16 + ((z + step + 8) % 8) * 2 + yh

    def along_x(step, flip):
        return ((x + step + 4) % 4) * 16 + z * 2 + yh + flip * (1 - 2 * yh)

    on_z = (along_z(1), along_z(-1), along_z(2), along_z(-2))
    on_x = (along_x(1, 0), along_x(-1, 0), along_x(2, 0), along_x(0, 1))
    k1, k2, k3, k4 = ((c * a + (1 - c) * b, t) for a, b in zip(on_z, on_x))
    q1, q2, q3, q4 = ((c * b + (1 - c) * a, t) for a, b in zip(on_z, on_x))
    t_sib = yl * 2 + 1 - c
    t_part = (1 - yl) * 2 + c
    t_cross = (1 - yl) * 2 + 1 - c
    t_far0 = (1 - yl) * 2
    t_far1 = (1 - yl) * 2 + 1
    p_flip = p + 1 - 2 * yh
    sibling = (p, t_sib)
    partner = (p, t_part)

    barrier = pltpu.get_barrier_semaphore()
    greeted = [sibling, (p, t_far0), (p, t_far1), (p_flip, t_far0), (p_flip, t_far1)]
    greeted += [(along_z(step), t) for step in Z_STEP.values()]
    greeted += [(along_x(*step), t) for step in X_STEP.values()]
    for device in greeted:
        pl.semaphore_signal(barrier, inc=1, device_id=device, device_id_type=pl.DeviceIdType.MESH)

    local = []

    def fetch(src, dst):
        copy = pltpu.make_async_copy(src, dst, lsem.at[len(local)])
        copy.start()
        local.append(copy)
        return copy

    own_video = fetch(video, vb.at[t])
    own_copies = [
        fetch(sk, kb.at[pl.ds(OWN_STALE, ROWS)]),
        fetch(sv, vvb.at[pl.ds(OWN_STALE, ROWS)]),
    ]
    text_copies = [fetch(tk, kb.at[pl.ds(0, TEXT)]), fetch(tv, vvb.at[pl.ds(0, TEXT)])]
    got_wq = fetch(wq, wqb)
    got_wk = fetch(wk, wkv.at[:, pl.ds(0, WIDTH)])
    got_wv = fetch(wv, wkv.at[:, pl.ds(WIDTH, WIDTH)])
    got_wo = fetch(wout.at[:, pl.ds(pl.multiple_of(t * FEAT, FEAT), FEAT)], wob.at[t])

    def spread(r, carry):
        posb[pl.ds(r, 1), :] = jnp.full((1, HEAD_DIM), pos[r], jnp.int32)
        return carry

    lax.fori_loop(0, ROWS, spread, 0)
    place = posb[...].astype(f32)
    frame = jnp.floor((place + 0.5) * (1.0 / 3600.0))
    within = place - 3600.0 * frame
    high = jnp.floor((within + 0.5) * (1.0 / 80.0))
    across = within - 80.0 * high
    lane = lax.broadcasted_iota(jnp.int32, (ROWS, HEAD_DIM), 1)
    angle = jnp.where(lane < 16, frame, jnp.where(lane < 72, high, across)) * rates[...]
    even = lane % 2 == 0
    cosb[...] = jnp.cos(angle)
    sine = jnp.sin(angle)
    sinb[...] = jnp.where(even, -sine, sine)
    stp[...] = jnp.zeros(stp.shape, f32)

    pl.semaphore_wait(barrier, len(greeted))

    sent = []

    def send(src, dst, recv, device):
        index = len(sent)

        def make():
            return pltpu.make_async_remote_copy(
                src_ref=src() if callable(src) else src, dst_ref=dst() if callable(dst) else dst,
                send_sem=ssem.at[index], recv_sem=rsem.at[recv],
                device_id=device, device_id_type=pl.DeviceIdType.MESH,
            )

        sent.append(make)
        make().start()

    def arrived(dst, recv):
        pltpu.make_async_copy(dst, dst, rsem.at[recv]).wait()

    for half, (r0, n) in enumerate(HALVES):
        send(video.at[pl.ds(r0, n)], vb.at[t, pl.ds(r0, n)], R_PART + half, partner)
    for half, (r0, n) in enumerate(HALVES):
        send(video.at[pl.ds(r0, n)], vb.at[t, pl.ds(r0, n)], R_SIB + half, sibling)

    def place_of(slot):
        return NEAR + (slot - 1) * ROWS if slot < 5 else FAR + (slot - 5) * ROWS

    def kv_slot(buffer, slot):
        return buffer.at[pl.ds(place_of(slot), ROWS)]

    def kv_arrived(slot):
        arrived(kv_slot(kb, slot), R_KV + 2 * slot)
        arrived(kv_slot(vvb, slot), R_KV + 2 * slot + 1)

    def kv_send(buffer, which, row, slot, device):
        src = buffer.at[pl.ds(pl.multiple_of(row, 16), ROWS)]
        send(src, kv_slot(buffer, slot), R_KV + 2 * slot + which, device)

    for which, own in enumerate((sk, sv)):
        buffer = (kb, vvb)[which]
        send(own, kv_slot(buffer, 1), R_KV + 2 + which, k1)
        send(own, kv_slot(buffer, 2), R_KV + 4 + which, k2)

    def normalise(r0, n):
        blocks = [vb[f, r0 : r0 + n, :].astype(f32) for f in range(4)]
        mean = sum(jnp.sum(b, axis=1, keepdims=True) for b in blocks) * (1.0 / D)
        spread = sum(jnp.sum((b - mean) ** 2, axis=1, keepdims=True) for b in blocks) * (1.0 / D)
        rstd = lax.rsqrt(spread + EPSILON)
        for f in range(4):
            cols = slice(f * FEAT, (f + 1) * FEAT)
            nb[r0 : r0 + n, cols] = (
                (blocks[f] - mean) * rstd * (1.0 + scale[:, cols]) + shift[:, cols]
            ).astype(bf16)

    def rows_of(slot, half):
        r0, n = HALVES[half]
        return vb.at[slot, pl.ds(r0, n)]

    far_a = c * place_of(3) + (1 - c) * place_of(4)
    near_a = c * place_of(1) + (1 - c) * OWN_STALE
    near_b = c * place_of(2) + (1 - c) * OWN_STALE
    to_a = (c * k1[0] + (1 - c) * k3[0], t)
    to_b = (c * k2[0] + (1 - c) * k4[0], t)

    def second_round(which):
        buffer = (kb, vvb)[which]
        for slot in (1, 2):
            arrived(kv_slot(buffer, slot), R_KV + 2 * slot + which)
        kv_send(buffer, which, near_a, 3, to_a)
        kv_send(buffer, which, near_b, 4, to_b)

    def third_round(which):
        buffer = (kb, vvb)[which]
        for slot in (3, 4):
            arrived(kv_slot(buffer, slot), R_KV + 2 * slot + which)
        kv_send(buffer, which, far_a, 5, k1)
        kv_send(buffer, which, place_of(4), 6, k2)
        if which == 0:
            kv_send(buffer, which, far_a, 7, k3)
        else:
            kv_send(buffer, which, place_of(4), 7, (c * k4[0] + (1 - c) * k3[0], t))

    def pass_features(half):
        arrived(rows_of(t_part, half), R_PART + half)
        send(rows_of(t_part, half), rows_of(t_part, half), R_FWD + half, sibling)

    def normalise_half(half):
        arrived(rows_of(t_sib, half), R_SIB + half)
        arrived(rows_of(t_cross, half), R_FWD + half)
        normalise(*HALVES[half])

    own_video.wait()
    for copy in own_copies:
        copy.wait()
    second_round(0)
    pass_features(0)
    second_round(1)
    third_round(0)
    pass_features(1)
    normalise_half(0)
    third_round(1)
    normalise_half(1)

    def turned(flat, gain, target):
        for h in range(LOCAL_HEADS):
            hs = slice(h * HEAD_DIM, (h + 1) * HEAD_DIM)
            v = flat[:, hs]
            v = v * lax.rsqrt(jnp.mean(v * v, axis=1, keepdims=True) + EPSILON) * gain[...]
            other = jnp.where(even, pltpu.roll(v, HEAD_DIM - 1, 1), pltpu.roll(v, 1, 1))
            target[:, hs] = (v * cosb[...] + other * sinb[...]).astype(bf16)

    got_wq.wait()
    turned(jnp.dot(nb[...], wqb[...], preferred_element_type=f32), q_gain, qb.at[0])
    for slot, device in ((1, q1), (2, q2), (3, q3), (4, q4)):
        send(qb.at[0], qb.at[slot], R_Q + slot, device)

    got_wk.wait()
    got_wv.wait()
    flat = jnp.dot(nb[...], wkv[...], preferred_element_type=f32)
    turned(flat[:, 0:WIDTH], k_gain, kb.at[pl.ds(FRESH, ROWS)])
    vvb[FRESH : FRESH + ROWS, :] = flat[:, WIDTH:].astype(bf16)
    out_k = fetch(kb.at[pl.ds(FRESH, ROWS)], fk)
    out_v = fetch(vvb.at[pl.ds(FRESH, ROWS)], fv)
    for copy in text_copies:
        copy.wait()

    def heads(h):
        return slice(h * HEAD_DIM, (h + 1) * HEAD_DIM)

    def tiles(array):
        return [
            array[:, i : min(i + HEAD_DIM, array.shape[1])] for i in range(0, array.shape[1], HEAD_DIM)
        ]

    def join(op, wide, tile):
        n = tile.shape[1]
        if n == HEAD_DIM:
            return op(wide, tile)
        return jnp.concatenate([op(wide[:, :n], tile), wide[:, n:]], axis=1)

    def row_top(scores):
        parts = tiles(scores)
        top = parts[0]
        for part in parts[1:]:
            top = join(jnp.maximum, top, part)
        return jnp.broadcast_to(jnp.max(top, axis=1, keepdims=True), (ROWS, HEAD_DIM))

    def weigh(scores, top, total):
        weights = [
            jnp.exp2((part - top[:, : part.shape[1]]) * EXP_FACTOR) for part in tiles(scores)
        ]
        for part in weights:
            total = join(jnp.add, total, part)
        return jnp.concatenate([part.astype(bf16) for part in weights], axis=1), total

    def scores_of(j, h, k0, n):
        return lax.dot_general(
            qb[j, :, heads(h)], kb[pl.ds(k0, n), heads(h)], (((1,), (1,)), ((), ())),
            preferred_element_type=f32,
        )

    def product(weights, h, k0, n):
        return jnp.dot(weights, vvb[pl.ds(k0, n), heads(h)], preferred_element_type=f32)

    live = lax.broadcasted_iota(jnp.int32, (1, TEXT), 1) < count[0]
    for h in range(LOCAL_HEADS):
        scores = jnp.where(live, scores_of(0, h, 0, TEXT), -1e30)
        top = row_top(scores)
        weights, total = weigh(scores, top, jnp.zeros((ROWS, HEAD_DIM), f32))
        ob[0, :, heads(h)] = product(weights, h, 0, TEXT)
        tops[0, h] = top
        sums[0, h] = total

    def q_arrived(slot):
        arrived(qb.at[slot], R_Q + slot)

    def half_step(j, k0, span, first):
        def held(empty, state):
            return state if first is False else jnp.where(first, empty, state)

        def score(h):
            scores = scores_of(j, h, k0, span)
            sb[h % 2, :, 0:span] = scores
            return row_top(scores)

        seen = score(0)
        for h in range(LOCAL_HEADS):
            before = held(-1e30, tops[j, h])
            top = jnp.maximum(before, seen)
            old = jnp.exp2((before - top) * EXP_FACTOR)
            if h + 1 < LOCAL_HEADS:
                seen = score(h + 1)
            weights, total = weigh(sb[h % 2, :, 0:span], top, held(0.0, sums[j, h]) * old)
            ob[j, :, heads(h)] = (
                held(0.0, ob[j, :, heads(h)]) * old + product(weights, h, k0, span)
            )
            tops[j, h] = top
            sums[j, h] = total

    column = lax.broadcasted_iota(jnp.int32, (ROWS, HEAD_DIM), 1)

    def pack(j):
        stats = jnp.zeros((ROWS, HEAD_DIM), f32)
        for h in range(LOCAL_HEADS):
            stats = jnp.where(column == h, tops[j, h], stats)
            stats = jnp.where(column == 3 + h, jnp.sum(sums[j, h], axis=1, keepdims=True), stats)
        stp[0:ROWS, :] = stats
        ss[j] = jnp.transpose(stp[...])[0:8, :]

    def give_back(j, device):
        return [
            pltpu.make_async_remote_copy(
                src_ref=source.at[j], dst_ref=target.at[j], send_sem=osem.at[2 * j + k],
                recv_sem=rsem.at[R_RS + 2 * j + k], device_id=device, device_id_type=pl.DeviceIdType.MESH,
            )
            for k, (source, target) in enumerate(((so, ro), (ss, rs)))
        ]

    far_q = (1 - c) * 3 + c * 4
    wo_recv = R_WO + t
    q_last = ((1 - c) * q4[0] + c * q3[0], t)

    def step(i, codes):
        slots, parts, z_steps, x_steps, group = codes
        n = group * 8 + i
        j = slots % 8
        part = parts % 2

        for when, slot in ((1, 1), (2, 2), (9, 5), (11, 6)):
            pl.when(n == when)(functools.partial(q_arrived, slot))

        @pl.when(n == 3)
        def _():
            q_arrived(3)
            q_arrived(4)
            send(lambda: qb.at[far_q], lambda: qb.at[5], R_Q + 5, q1)
            send(lambda: qb.at[4], lambda: qb.at[6], R_Q + 6, q2)
            for half, (source, device) in enumerate(((far_q, q3), (4, q_last))):
                r0, rows = HALVES[half]
                send(
                    lambda source=source, r0=r0, rows=rows: qb.at[source, pl.ds(r0, rows)],
                    lambda r0=r0, rows=rows: qb.at[7, pl.ds(r0, rows)], R_Q + 7 + half, device,
                )

        @pl.when(n == 13)
        def _():
            for half, (r0, rows) in enumerate(HALVES):
                arrived(qb.at[7, pl.ds(r0, rows)], R_Q + 7 + half)

        @pl.when(n == 5)
        def _():
            for slot in (5, 6, 7):
                kv_arrived(slot)
            for user, device in ((t_sib, sibling), (t_far0, (p, t_far0)), (t_far1, (p_flip, t_far1))):
                send(
                    lambda user=user: wout.at[:, pl.ds(pl.multiple_of(user * FEAT, FEAT), FEAT)],
                    lambda: wob.at[t], wo_recv, device,
                )

        @pl.when(part == 0)
        def _():
            k0 = FRESH + ((n + 15) // 16) * ROWS
            half_step(j, pl.multiple_of(k0, 16), FIRST_SPAN, n > 0)

        @pl.when(part == 1)
        def _():
            half_step(j, FAR, LATER_SPAN, False)

        @pl.when(part == 1)
        def _():
            pack(j)

        @pl.when(jnp.logical_and(part == 1, n < 15))
        def _():
            so[j] = ob[j].astype(bf16)
            shift_z = z_steps % 8 - 3
            shift_x = x_steps % 4 - 1
            flip = (x_steps // 4) % 2
            owner = (1 - c) * along_z(shift_z) + c * along_x(shift_x, flip)
            for copy in give_back(j, (owner, t)):
                copy.start()

        return slots // 8, parts // 2, z_steps // 8, x_steps // 8, group

    first_codes, later_codes = step_codes(0), step_codes(8)

    def eight(group, carry):
        codes = tuple(a + group * (b - a) for a, b in zip(first_codes, later_codes))
        lax.fori_loop(0, 8, step, codes + (group,))
        return carry

    lax.fori_loop(0, 2, eight, 0)

    for slot in range(1, 8):
        arrived(ro.at[slot], R_RS + 2 * slot)
        arrived(rs.at[slot], R_RS + 2 * slot + 1)
    stats = [ss[0]] + [rs[slot] for slot in range(1, 8)]
    top = stats[0][0:3]
    for part in stats[1:]:
        top = jnp.maximum(top, part[0:3])
    shares = [jnp.exp2((part[0:3] - top) * EXP_FACTOR) for part in stats]
    total = sum(share * part[3:6] for share, part in zip(shares, stats))
    blank = jnp.zeros((5, 384), f32)
    rows = [jnp.concatenate([share / total, blank], axis=0) for share in shares]
    rows.append(jnp.zeros((64, 384), f32))
    weight = jnp.transpose(jnp.concatenate(rows, axis=0))[0:ROWS]
    for h in range(LOCAL_HEADS):
        summed = ob[0, :, heads(h)] * weight[:, h : h + 1]
        for slot in range(1, 8):
            summed += ro[slot, :, heads(h)].astype(f32) * weight[:, 8 * slot + h : 8 * slot + h + 1]
        atb[t, :, heads(h)] = summed.astype(bf16)

    send(atb.at[t], atb.at[t], R_ATT + 1, partner)
    send(atb.at[t], atb.at[t], R_ATT, sibling)
    got_wo.wait()
    for slot in (t_sib, t_far0, t_far1):
        arrived(wob.at[slot], R_WO + slot)

    def term(slot):
        return jnp.dot(atb[slot], wob[slot], preferred_element_type=f32)

    branch = term(t)
    arrived(atb.at[t_sib], R_ATT)
    branch = branch + term(t_sib)
    arrived(atb.at[t_part], R_ATT + 1)
    send(atb.at[t_part], atb.at[t_part], R_ATT + 2, sibling)
    branch = branch + term(t_part)
    arrived(atb.at[t_cross], R_ATT + 2)
    branch = branch + term(t_cross)
    mixed[...] = vb[t].astype(f32) + gate[...][None, :] * branch

    out_k.wait()
    out_v.wait()
    for make in sent:
        make().wait_send()
    for slot in range(1, 8):
        for copy in give_back(slot, (p, t_sib)):
            copy.wait_send()


def hand_over(*refs):
    sources, targets, held, sems = refs[:3], refs[3:6], refs[6:9], refs[9]
    inward = [pltpu.make_async_copy(a, b, sems.at[i]) for i, (a, b) in enumerate(zip(sources, held))]
    outward = [
        pltpu.make_async_copy(a, b, sems.at[3 + i]) for i, (a, b) in enumerate(zip(held, targets))
    ]
    for copy in inward:
        copy.start()
    for first, second in zip(inward, outward):
        first.wait()
        second.start()
    for copy in outward:
        copy.wait()


def shards(
    video, positions, text_count, mod_shift, mod_scale, gate, w_query, w_key, w_value, w_out,
    q_gain, k_gain, stale_keys, stale_values, text_keys, text_values,
):
    bf16, f32 = jnp.bfloat16, jnp.float32
    vmem = pl.BlockSpec(memory_space=pltpu.VMEM)
    smem = pl.BlockSpec(memory_space=pltpu.SMEM)
    hbm = pl.BlockSpec(memory_space=pl.ANY)
    outs = (
        jax.ShapeDtypeStruct((ROWS, FEAT), f32),
        jax.ShapeDtypeStruct((ROWS, WIDTH), bf16),
        jax.ShapeDtypeStruct((ROWS, WIDTH), bf16),
    )
    made = pl.pallas_call(
        kernel,
        out_shape=outs,
        in_specs=[
            hbm, smem, smem, vmem, vmem, vmem, hbm, hbm, hbm, hbm, vmem, vmem, hbm, hbm, hbm, hbm,
            vmem,
        ],
        out_specs=(vmem, hbm, hbm),
        scratch_shapes=[
            pltpu.VMEM((4, ROWS, FEAT), bf16),
            pltpu.VMEM((ROWS, D), bf16),
            pltpu.VMEM((D, WIDTH), bf16),
            pltpu.VMEM((D, 2 * WIDTH), bf16),
            pltpu.VMEM((KEYS, WIDTH), bf16),
            pltpu.VMEM((KEYS, WIDTH), bf16),
            pltpu.VMEM((8, ROWS, WIDTH), bf16),
            pltpu.VMEM((ROWS, HEAD_DIM), jnp.int32),
            pltpu.VMEM((ROWS, HEAD_DIM), f32),
            pltpu.VMEM((ROWS, HEAD_DIM), f32),
            pltpu.VMEM((2, ROWS, FIRST_SPAN), f32),
            pltpu.VMEM((8, ROWS, WIDTH), f32),
            pltpu.VMEM((8, LOCAL_HEADS, ROWS, HEAD_DIM), f32),
            pltpu.VMEM((8, LOCAL_HEADS, ROWS, HEAD_DIM), f32),
            pltpu.VMEM((384, HEAD_DIM), f32),
            pltpu.VMEM((8, ROWS, WIDTH), bf16),
            pltpu.VMEM((8, 8, 384), f32),
            pltpu.VMEM((8, ROWS, WIDTH), bf16),
            pltpu.VMEM((8, 8, 384), f32),
            pltpu.VMEM((4, WIDTH, FEAT), bf16),
            pltpu.VMEM((4, ROWS, WIDTH), bf16),
            pltpu.SemaphoreType.DMA((N_SEND,)),
            pltpu.SemaphoreType.DMA((16,)),
            pltpu.SemaphoreType.DMA((N_RECV,)),
            pltpu.SemaphoreType.DMA((N_LOCAL,)),
        ],
        compiler_params=pltpu.CompilerParams(
            collective_id=0, has_side_effects=True, vmem_limit_bytes=60 * 1024 * 1024
        ),
        name="attention_half",
    )(
        video,
        positions,
        text_count,
        mod_shift.reshape(1, D),
        mod_scale.reshape(1, D),
        gate,
        w_query,
        w_key,
        w_value,
        w_out,
        q_gain.reshape(1, HEAD_DIM),
        k_gain.reshape(1, HEAD_DIM),
        stale_keys,
        stale_values,
        text_keys,
        text_values,
        jnp.asarray(pair_rates()),
    )
    return pl.pallas_call(
        hand_over,
        out_shape=outs,
        in_specs=[hbm] * 3,
        out_specs=(hbm,) * 3,
        scratch_shapes=[pltpu.VMEM(out.shape, out.dtype) for out in outs]
        + [pltpu.SemaphoreType.DMA((6,))],
        compiler_params=pltpu.CompilerParams(vmem_limit_bytes=60 * 1024 * 1024),
        name="hand_over",
    )(*made)


def solution(mesh):
    return jax.shard_map(
        shards,
        mesh=mesh,
        in_specs=(
            P("patch", "tensor"),
            P("patch"),
            P(),
            P(),
            P(),
            P("tensor"),
            P(None, "tensor"),
            P(None, "tensor"),
            P(None, "tensor"),
            P("tensor", None),
            P(),
            P(),
            P("patch", "tensor"),
            P("patch", "tensor"),
            P(None, "tensor"),
            P(None, "tensor"),
        ),
        out_specs=(P("patch", "tensor"), P("patch", "tensor"), P("patch", "tensor")),
        check_vma=False,
    )
```

```python
import functools
import math

import jax
import jax.numpy as jnp
import numpy as np
from jax import lax
from jax.experimental import pallas as pl
from jax.experimental.pallas import tpu as pltpu
from jax.sharding import PartitionSpec as P

D = 3072
HEAD_DIM = 128
LOCAL_HEADS = 3
ROWS = 272
WIDTH = LOCAL_HEADS * HEAD_DIM
FEAT = 768
TEXT = 256
EPSILON = 1e-06
EXP_FACTOR = math.log2(math.e) / math.sqrt(HEAD_DIM)

FRESH = TEXT
NEAR = FRESH + ROWS
OWN_STALE = NEAR + 4 * ROWS
FAR = OWN_STALE + ROWS
KEYS = FAR + 3 * ROWS
FIRST_SPAN = 5 * ROWS
LATER_SPAN = 3 * ROWS

HALVES = ((0, 144), (144, 128))

STEPS = (
    (0, 0), (1, 0), (2, 0), (3, 0), (4, 0), (1, 1), (2, 1), (3, 1),
    (4, 1), (5, 0), (5, 1), (6, 0), (6, 1), (7, 0), (7, 1), (0, 1),
)
Z_STEP = {1: -1, 2: 1, 3: -2, 4: 2, 5: -3, 6: 3, 7: 4}
X_STEP = {1: (-1, 0), 2: (1, 0), 3: (2, 0), 4: (0, 1), 5: (-1, 1), 6: (1, 1), 7: (2, 1)}


def digits(values, base):
    total = 0
    for value in reversed(values):
        total = total * base + value
    return total


def step_codes(first):
    part = STEPS[first : first + 8]
    return (
        digits([slot for slot, _ in part], 8),
        digits([half for _, half in part], 2),
        digits([Z_STEP.get(slot, 0) + 3 for slot, _ in part], 8),
        digits([X_STEP.get(slot, (0, 0))[0] + 1 + 4 * X_STEP.get(slot, (0, 0))[1] for slot, _ in part], 8),
    )


R_SIB, R_PART, R_FWD, R_KV, R_Q, R_WO, R_RS, R_ATT = 0, 2, 4, 6, 22, 31, 35, 51
N_RECV = 57
N_SEND = 64
N_LOCAL = 16


def pair_rates():
    pairs = HEAD_DIM // 2
    frame = HEAD_DIM // 16
    high = (pairs - frame) // 2
    wide = pairs - frame - high
    rates = np.concatenate(
        [256.0 ** (-np.arange(n, dtype=np.float64) / n) for n in (frame, high, wide)]
    )
    return np.repeat(rates, 2).astype(np.float32)[None, :]


def kernel(
    video, pos, count, shift, scale, gate, wq, wk, wv, wout, q_gain, k_gain, sk, sv, tk, tv, rates,
    mixed, fk, fv,
    vb, nb, wqb, wkv, kb, vvb, qb, posb, cosb, sinb, sb, ob, tops, sums, stp, so, ss, ro, rs, wob, atb,
    ssem, osem, rsem, lsem,
):
    f32 = jnp.float32
    bf16 = jnp.bfloat16
    p = lax.axis_index("patch")
    t = lax.axis_index("tensor")
    x = p // 16
    z = (p // 2) % 8
    yh = p % 2
    yl = t // 2
    c = t % 2

    def along_z(step):
        return x * 16 + ((z + step + 8) % 8) * 2 + yh

    def along_x(step, flip):
        return ((x + step + 4) % 4) * 16 + z * 2 + yh + flip * (1 - 2 * yh)

    on_z = (along_z(1), along_z(-1), along_z(2), along_z(-2))
    on_x = (along_x(1, 0), along_x(-1, 0), along_x(2, 0), along_x(0, 1))
    k1, k2, k3, k4 = ((c * a + (1 - c) * b, t) for a, b in zip(on_z, on_x))
    q1, q2, q3, q4 = ((c * b + (1 - c) * a, t) for a, b in zip(on_z, on_x))
    t_sib = yl * 2 + 1 - c
    t_part = (1 - yl) * 2 + c
    t_cross = (1 - yl) * 2 + 1 - c
    t_far0 = (1 - yl) * 2
    t_far1 = (1 - yl) * 2 + 1
    p_flip = p + 1 - 2 * yh
    sibling = (p, t_sib)
    partner = (p, t_part)

    barrier = pltpu.get_barrier_semaphore()
    greeted = [sibling, (p, t_far0), (p, t_far1), (p_flip, t_far0), (p_flip, t_far1)]
    greeted += [(along_z(step), t) for step in Z_STEP.values()]
    greeted += [(along_x(*step), t) for step in X_STEP.values()]
    for device in greeted:
        pl.semaphore_signal(barrier, inc=1, device_id=device, device_id_type=pl.DeviceIdType.MESH)

    local = []

    def fetch(src, dst):
        copy = pltpu.make_async_copy(src, dst, lsem.at[len(local)])
        copy.start()
        local.append(copy)
        return copy

    own_video = fetch(video, vb.at[t])
    own_copies = [
        fetch(sk, kb.at[pl.ds(OWN_STALE, ROWS)]),
        fetch(sv, vvb.at[pl.ds(OWN_STALE, ROWS)]),
    ]
    text_copies = [fetch(tk, kb.at[pl.ds(0, TEXT)]), fetch(tv, vvb.at[pl.ds(0, TEXT)])]
    got_wq = fetch(wq, wqb)
    got_wk = fetch(wk, wkv.at[:, pl.ds(0, WIDTH)])
    got_wv = fetch(wv, wkv.at[:, pl.ds(WIDTH, WIDTH)])
    got_wo = fetch(wout.at[:, pl.ds(pl.multiple_of(t * FEAT, FEAT), FEAT)], wob.at[t])

    def spread(r, carry):
        posb[pl.ds(r, 1), :] = jnp.full((1, HEAD_DIM), pos[r], jnp.int32)
        return carry

    lax.fori_loop(0, ROWS, spread, 0)
    place = posb[...].astype(f32)
    frame = jnp.floor((place + 0.5) * (1.0 / 3600.0))
    within = place - 3600.0 * frame
    high = jnp.floor((within + 0.5) * (1.0 / 80.0))
    across = within - 80.0 * high
    lane = lax.broadcasted_iota(jnp.int32, (ROWS, HEAD_DIM), 1)
    angle = jnp.where(lane < 16, frame, jnp.where(lane < 72, high, across)) * rates[...]
    even = lane % 2 == 0
    cosb[...] = jnp.cos(angle)
    sine = jnp.sin(angle)
    sinb[...] = jnp.where(even, -sine, sine)
    stp[...] = jnp.zeros(stp.shape, f32)

    pl.semaphore_wait(barrier, len(greeted))

    sent = []

    def send(src, dst, recv, device):
        index = len(sent)

        def make():
            return pltpu.make_async_remote_copy(
                src_ref=src() if callable(src) else src, dst_ref=dst() if callable(dst) else dst,
                send_sem=ssem.at[index], recv_sem=rsem.at[recv],
                device_id=device, device_id_type=pl.DeviceIdType.MESH,
            )

        sent.append(make)
        make().start()

    def arrived(dst, recv):
        pltpu.make_async_copy(dst, dst, rsem.at[recv]).wait()

    for half, (r0, n) in enumerate(HALVES):
        send(video.at[pl.ds(r0, n)], vb.at[t, pl.ds(r0, n)], R_PART + half, partner)
    for half, (r0, n) in enumerate(HALVES):
        send(video.at[pl.ds(r0, n)], vb.at[t, pl.ds(r0, n)], R_SIB + half, sibling)

    def place_of(slot):
        return NEAR + (slot - 1) * ROWS if slot < 5 else FAR + (slot - 5) * ROWS

    def kv_slot(buffer, slot):
        return buffer.at[pl.ds(place_of(slot), ROWS)]

    def kv_arrived(slot):
        arrived(kv_slot(kb, slot), R_KV + 2 * slot)
        arrived(kv_slot(vvb, slot), R_KV + 2 * slot + 1)

    def kv_send(buffer, which, row, slot, device):
        src = buffer.at[pl.ds(pl.multiple_of(row, 16), ROWS)]
        send(src, kv_slot(buffer, slot), R_KV + 2 * slot + which, device)

    for which, own in enumerate((sk, sv)):
        buffer = (kb, vvb)[which]
        send(own, kv_slot(buffer, 1), R_KV + 2 + which, k1)
        send(own, kv_slot(buffer, 2), R_KV + 4 + which, k2)

    def normalise(r0, n):
        blocks = [vb[f, r0 : r0 + n, :].astype(f32) for f in range(4)]
        mean = sum(jnp.sum(b, axis=1, keepdims=True) for b in blocks) * (1.0 / D)
        spread = sum(jnp.sum((b - mean) ** 2, axis=1, keepdims=True) for b in blocks) * (1.0 / D)
        rstd = lax.rsqrt(spread + EPSILON)
        for f in range(4):
            cols = slice(f * FEAT, (f + 1) * FEAT)
            nb[r0 : r0 + n, cols] = (
                (blocks[f] - mean) * rstd * (1.0 + scale[:, cols]) + shift[:, cols]
            ).astype(bf16)

    def rows_of(slot, half):
        r0, n = HALVES[half]
        return vb.at[slot, pl.ds(r0, n)]

    far_a = c * place_of(3) + (1 - c) * place_of(4)
    near_a = c * place_of(1) + (1 - c) * OWN_STALE
    near_b = c * place_of(2) + (1 - c) * OWN_STALE
    to_a = (c * k1[0] + (1 - c) * k3[0], t)
    to_b = (c * k2[0] + (1 - c) * k4[0], t)

    def second_round(which):
        buffer = (kb, vvb)[which]
        for slot in (1, 2):
            arrived(kv_slot(buffer, slot), R_KV + 2 * slot + which)
        kv_send(buffer, which, near_a, 3, to_a)
        kv_send(buffer, which, near_b, 4, to_b)

    def third_round(which):
        buffer = (kb, vvb)[which]
        for slot in (3, 4):
            arrived(kv_slot(buffer, slot), R_KV + 2 * slot + which)
        kv_send(buffer, which, far_a, 5, k1)
        kv_send(buffer, which, place_of(4), 6, k2)
        if which == 0:
            kv_send(buffer, which, far_a, 7, k3)
        else:
            kv_send(buffer, which, place_of(4), 7, (c * k4[0] + (1 - c) * k3[0], t))

    def pass_features(half):
        arrived(rows_of(t_part, half), R_PART + half)
        send(rows_of(t_part, half), rows_of(t_part, half), R_FWD + half, sibling)

    def normalise_half(half):
        arrived(rows_of(t_sib, half), R_SIB + half)
        arrived(rows_of(t_cross, half), R_FWD + half)
        normalise(*HALVES[half])

    own_video.wait()
    for copy in own_copies:
        copy.wait()
    second_round(0)
    pass_features(0)
    second_round(1)
    third_round(0)
    pass_features(1)
    normalise_half(0)
    third_round(1)
    normalise_half(1)

    def turned(flat, gain, target):
        for h in range(LOCAL_HEADS):
            hs = slice(h * HEAD_DIM, (h + 1) * HEAD_DIM)
            v = flat[:, hs]
            v = v * lax.rsqrt(jnp.mean(v * v, axis=1, keepdims=True) + EPSILON) * gain[...]
            other = jnp.where(even, pltpu.roll(v, HEAD_DIM - 1, 1), pltpu.roll(v, 1, 1))
            target[:, hs] = (v * cosb[...] + other * sinb[...]).astype(bf16)

    got_wq.wait()
    turned(jnp.dot(nb[...], wqb[...], preferred_element_type=f32), q_gain, qb.at[0])
    for slot, device in ((1, q1), (2, q2), (3, q3), (4, q4)):
        send(qb.at[0], qb.at[slot], R_Q + slot, device)

    got_wk.wait()
    got_wv.wait()
    flat = jnp.dot(nb[...], wkv[...], preferred_element_type=f32)
    turned(flat[:, 0:WIDTH], k_gain, kb.at[pl.ds(FRESH, ROWS)])
    vvb[FRESH : FRESH + ROWS, :] = flat[:, WIDTH:].astype(bf16)
    out_k = fetch(kb.at[pl.ds(FRESH, ROWS)], fk)
    out_v = fetch(vvb.at[pl.ds(FRESH, ROWS)], fv)
    for copy in text_copies:
        copy.wait()

    def heads(h):
        return slice(h * HEAD_DIM, (h + 1) * HEAD_DIM)

    def tiles(array):
        return [
            array[:, i : min(i + HEAD_DIM, array.shape[1])] for i in range(0, array.shape[1], HEAD_DIM)
        ]

    def join(op, wide, tile):
        n = tile.shape[1]
        if n == HEAD_DIM:
            return op(wide, tile)
        return jnp.concatenate([op(wide[:, :n], tile), wide[:, n:]], axis=1)

    def row_top(scores):
        parts = tiles(scores)
        top = parts[0]
        for part in parts[1:]:
            top = join(jnp.maximum, top, part)
        return jnp.broadcast_to(jnp.max(top, axis=1, keepdims=True), (ROWS, HEAD_DIM))

    def weigh(scores, top, total):
        weights = [
            jnp.exp2((part - top[:, : part.shape[1]]) * EXP_FACTOR) for part in tiles(scores)
        ]
        for part in weights:
            total = join(jnp.add, total, part)
        return jnp.concatenate([part.astype(bf16) for part in weights], axis=1), total

    def scores_of(j, h, k0, n):
        return lax.dot_general(
            qb[j, :, heads(h)], kb[pl.ds(k0, n), heads(h)], (((1,), (1,)), ((), ())),
            preferred_element_type=f32,
        )

    def product(weights, h, k0, n):
        return jnp.dot(weights, vvb[pl.ds(k0, n), heads(h)], preferred_element_type=f32)

    live = lax.broadcasted_iota(jnp.int32, (1, TEXT), 1) < count[0]
    for h in range(LOCAL_HEADS):
        scores = jnp.where(live, scores_of(0, h, 0, TEXT), -1e30)
        top = row_top(scores)
        weights, total = weigh(scores, top, jnp.zeros((ROWS, HEAD_DIM), f32))
        ob[0, :, heads(h)] = product(weights, h, 0, TEXT)
        tops[0, h] = top
        sums[0, h] = total

    def q_arrived(slot):
        arrived(qb.at[slot], R_Q + slot)

    def half_step(j, k0, span, first):
        def held(empty, state):
            return state if first is False else jnp.where(first, empty, state)

        def score(h):
            scores = scores_of(j, h, k0, span)
            sb[h % 2, :, 0:span] = scores
            return row_top(scores)

        seen = score(0)
        for h in range(LOCAL_HEADS):
            before = held(-1e30, tops[j, h])
            top = jnp.maximum(before, seen)
            old = jnp.exp2((before - top) * EXP_FACTOR)
            if h + 1 < LOCAL_HEADS:
                seen = score(h + 1)
            weights, total = weigh(sb[h % 2, :, 0:span], top, held(0.0, sums[j, h]) * old)
            ob[j, :, heads(h)] = (
                held(0.0, ob[j, :, heads(h)]) * old + product(weights, h, k0, span)
            )
            tops[j, h] = top
            sums[j, h] = total

    column = lax.broadcasted_iota(jnp.int32, (ROWS, HEAD_DIM), 1)

    def pack(j):
        stats = jnp.zeros((ROWS, HEAD_DIM), f32)
        for h in range(LOCAL_HEADS):
            stats = jnp.where(column == h, tops[j, h], stats)
            stats = jnp.where(column == 3 + h, jnp.sum(sums[j, h], axis=1, keepdims=True), stats)
        stp[0:ROWS, :] = stats
        ss[j] = jnp.transpose(stp[...])[0:8, :]

    def give_back(j, device):
        return [
            pltpu.make_async_remote_copy(
                src_ref=source.at[j], dst_ref=target.at[j], send_sem=osem.at[2 * j + k],
                recv_sem=rsem.at[R_RS + 2 * j + k], device_id=device, device_id_type=pl.DeviceIdType.MESH,
            )
            for k, (source, target) in enumerate(((so, ro), (ss, rs)))
        ]

    far_q = (1 - c) * 3 + c * 4
    wo_recv = R_WO + t
    q_last = ((1 - c) * q4[0] + c * q3[0], t)

    def step(i, codes):
        slots, parts, z_steps, x_steps, group = codes
        n = group * 8 + i
        j = slots % 8
        part = parts % 2

        for when, slot in ((1, 1), (2, 2), (9, 5), (11, 6)):
            pl.when(n == when)(functools.partial(q_arrived, slot))

        @pl.when(n == 3)
        def _():
            q_arrived(3)
            q_arrived(4)
            send(lambda: qb.at[far_q], lambda: qb.at[5], R_Q + 5, q1)
            send(lambda: qb.at[4], lambda: qb.at[6], R_Q + 6, q2)
            for half, (source, device) in enumerate(((far_q, q3), (4, q_last))):
                r0, rows = HALVES[half]
                send(
                    lambda source=source, r0=r0, rows=rows: qb.at[source, pl.ds(r0, rows)],
                    lambda r0=r0, rows=rows: qb.at[7, pl.ds(r0, rows)], R_Q + 7 + half, device,
                )

        @pl.when(n == 13)
        def _():
            for half, (r0, rows) in enumerate(HALVES):
                arrived(qb.at[7, pl.ds(r0, rows)], R_Q + 7 + half)

        @pl.when(n == 5)
        def _():
            for slot in (5, 6, 7):
                kv_arrived(slot)
            for user, device in ((t_sib, sibling), (t_far0, (p, t_far0)), (t_far1, (p_flip, t_far1))):
                send(
                    lambda user=user: wout.at[:, pl.ds(pl.multiple_of(user * FEAT, FEAT), FEAT)],
                    lambda: wob.at[t], wo_recv, device,
                )

        @pl.when(part == 0)
        def _():
            k0 = FRESH + ((n + 15) // 16) * ROWS
            half_step(j, pl.multiple_of(k0, 16), FIRST_SPAN, n > 0)

        @pl.when(part == 1)
        def _():
            half_step(j, FAR, LATER_SPAN, False)

        @pl.when(part == 1)
        def _():
            pack(j)

        @pl.when(jnp.logical_and(part == 1, n < 15))
        def _():
            so[j] = ob[j].astype(bf16)
            shift_z = z_steps % 8 - 3
            shift_x = x_steps % 4 - 1
            flip = (x_steps // 4) % 2
            owner = (1 - c) * along_z(shift_z) + c * along_x(shift_x, flip)
            for copy in give_back(j, (owner, t)):
                copy.start()

        return slots // 8, parts // 2, z_steps // 8, x_steps // 8, group

    first_codes, later_codes = step_codes(0), step_codes(8)

    def eight(group, carry):
        codes = tuple(a + group * (b - a) for a, b in zip(first_codes, later_codes))
        lax.fori_loop(0, 8, step, codes + (group,))
        return carry

    lax.fori_loop(0, 2, eight, 0)

    for slot in range(1, 8):
        arrived(ro.at[slot], R_RS + 2 * slot)
        arrived(rs.at[slot], R_RS + 2 * slot + 1)
    stats = [ss[0]] + [rs[slot] for slot in range(1, 8)]
    top = stats[0][0:3]
    for part in stats[1:]:
        top = jnp.maximum(top, part[0:3])
    shares = [jnp.exp2((part[0:3] - top) * EXP_FACTOR) for part in stats]
    total = sum(share * part[3:6] for share, part in zip(shares, stats))
    blank = jnp.zeros((5, 384), f32)
    rows = [jnp.concatenate([share / total, blank], axis=0) for share in shares]
    rows.append(jnp.zeros((64, 384), f32))
    weight = jnp.transpose(jnp.concatenate(rows, axis=0))[0:ROWS]
    for half, (r0, n) in enumerate(HALVES):
        rows_here = slice(r0, r0 + n)
        for h in range(LOCAL_HEADS):
            summed = ob[0, rows_here, heads(h)] * weight[rows_here, h : h + 1]
            for slot in range(1, 8):
                factor = weight[rows_here, 8 * slot + h : 8 * slot + h + 1]
                summed += ro[slot, rows_here, heads(h)].astype(f32) * factor
            atb[t, rows_here, heads(h)] = summed.astype(bf16)
        mine = atb.at[t, pl.ds(r0, n)]
        send(mine, mine, R_ATT + 2 + half, partner)
        send(mine, mine, R_ATT + half, sibling)

    got_wo.wait()
    for slot in (t_sib, t_far0, t_far1):
        arrived(wob.at[slot], R_WO + slot)

    def term(slot):
        return jnp.dot(atb[slot], wob[slot], preferred_element_type=f32)

    branch = term(t)
    for half, (r0, n) in enumerate(HALVES):
        arrived(atb.at[t_sib, pl.ds(r0, n)], R_ATT + half)
    branch = branch + term(t_sib)
    for half, (r0, n) in enumerate(HALVES):
        theirs = atb.at[t_part, pl.ds(r0, n)]
        arrived(theirs, R_ATT + 2 + half)
        send(theirs, theirs, R_ATT + 4 + half, sibling)
    branch = branch + term(t_part)
    for half, (r0, n) in enumerate(HALVES):
        arrived(atb.at[t_cross, pl.ds(r0, n)], R_ATT + 4 + half)
    branch = branch + term(t_cross)
    mixed[...] = vb[t].astype(f32) + gate[...][None, :] * branch

    out_k.wait()
    out_v.wait()
    for make in sent:
        make().wait_send()
    for slot in range(1, 8):
        for copy in give_back(slot, (p, t_sib)):
            copy.wait_send()


def hand_over(*refs):
    sources, targets, held, sems = refs[:3], refs[3:6], refs[6:9], refs[9]
    inward = [pltpu.make_async_copy(a, b, sems.at[i]) for i, (a, b) in enumerate(zip(sources, held))]
    outward = [
        pltpu.make_async_copy(a, b, sems.at[3 + i]) for i, (a, b) in enumerate(zip(held, targets))
    ]
    for copy in inward:
        copy.start()
    for first, second in zip(inward, outward):
        first.wait()
        second.start()
    for copy in outward:
        copy.wait()


def shards(
    video, positions, text_count, mod_shift, mod_scale, gate, w_query, w_key, w_value, w_out,
    q_gain, k_gain, stale_keys, stale_values, text_keys, text_values,
):
    bf16, f32 = jnp.bfloat16, jnp.float32
    vmem = pl.BlockSpec(memory_space=pltpu.VMEM)
    smem = pl.BlockSpec(memory_space=pltpu.SMEM)
    hbm = pl.BlockSpec(memory_space=pl.ANY)
    outs = (
        jax.ShapeDtypeStruct((ROWS, FEAT), f32),
        jax.ShapeDtypeStruct((ROWS, WIDTH), bf16),
        jax.ShapeDtypeStruct((ROWS, WIDTH), bf16),
    )
    made = pl.pallas_call(
        kernel,
        out_shape=outs,
        in_specs=[
            hbm, smem, smem, vmem, vmem, vmem, hbm, hbm, hbm, hbm, vmem, vmem, hbm, hbm, hbm, hbm,
            vmem,
        ],
        out_specs=(vmem, hbm, hbm),
        scratch_shapes=[
            pltpu.VMEM((4, ROWS, FEAT), bf16),
            pltpu.VMEM((ROWS, D), bf16),
            pltpu.VMEM((D, WIDTH), bf16),
            pltpu.VMEM((D, 2 * WIDTH), bf16),
            pltpu.VMEM((KEYS, WIDTH), bf16),
            pltpu.VMEM((KEYS, WIDTH), bf16),
            pltpu.VMEM((8, ROWS, WIDTH), bf16),
            pltpu.VMEM((ROWS, HEAD_DIM), jnp.int32),
            pltpu.VMEM((ROWS, HEAD_DIM), f32),
            pltpu.VMEM((ROWS, HEAD_DIM), f32),
            pltpu.VMEM((2, ROWS, FIRST_SPAN), f32),
            pltpu.VMEM((8, ROWS, WIDTH), f32),
            pltpu.VMEM((8, LOCAL_HEADS, ROWS, HEAD_DIM), f32),
            pltpu.VMEM((8, LOCAL_HEADS, ROWS, HEAD_DIM), f32),
            pltpu.VMEM((384, HEAD_DIM), f32),
            pltpu.VMEM((8, ROWS, WIDTH), bf16),
            pltpu.VMEM((8, 8, 384), f32),
            pltpu.VMEM((8, ROWS, WIDTH), bf16),
            pltpu.VMEM((8, 8, 384), f32),
            pltpu.VMEM((4, WIDTH, FEAT), bf16),
            pltpu.VMEM((4, ROWS, WIDTH), bf16),
            pltpu.SemaphoreType.DMA((N_SEND,)),
            pltpu.SemaphoreType.DMA((16,)),
            pltpu.SemaphoreType.DMA((N_RECV,)),
            pltpu.SemaphoreType.DMA((N_LOCAL,)),
        ],
        compiler_params=pltpu.CompilerParams(
            collective_id=0, has_side_effects=True, vmem_limit_bytes=60 * 1024 * 1024
        ),
        name="attention_half",
    )(
        video,
        positions,
        text_count,
        mod_shift.reshape(1, D),
        mod_scale.reshape(1, D),
        gate,
        w_query,
        w_key,
        w_value,
        w_out,
        q_gain.reshape(1, HEAD_DIM),
        k_gain.reshape(1, HEAD_DIM),
        stale_keys,
        stale_values,
        text_keys,
        text_values,
        jnp.asarray(pair_rates()),
    )
    return pl.pallas_call(
        hand_over,
        out_shape=outs,
        in_specs=[hbm] * 3,
        out_specs=(hbm,) * 3,
        scratch_shapes=[pltpu.VMEM(out.shape, out.dtype) for out in outs]
        + [pltpu.SemaphoreType.DMA((6,))],
        compiler_params=pltpu.CompilerParams(vmem_limit_bytes=60 * 1024 * 1024),
        name="hand_over",
    )(*made)


def solution(mesh):
    return jax.shard_map(
        shards,
        mesh=mesh,
        in_specs=(
            P("patch", "tensor"),
            P("patch"),
            P(),
            P(),
            P(),
            P("tensor"),
            P(None, "tensor"),
            P(None, "tensor"),
            P(None, "tensor"),
            P("tensor", None),
            P(),
            P(),
            P("patch", "tensor"),
            P("patch", "tensor"),
            P(None, "tensor"),
            P(None, "tensor"),
        ),
        out_specs=(P("patch", "tensor"), P("patch", "tensor"), P("patch", "tensor")),
        check_vma=False,
    )
```
